128 devices in a mesh: win: 8 (over y, core), chan: 16 (over z, x).
Axes of the slice: x: 4, y: 4, z: 4, core: 2. Of those that a mesh axis runs over, the one named last changes fastest.
Arguments:
- spectra: bfloat16 [8, 2048, 8192], P(None, ('chan', 'win')), may hold values from -40 to 40
- pair_remote: int32 [16, 4], P('chan'), may hold values from 0 to 15, as said below
- pair_count: int32 [16], P('chan'), may hold values from 0 to 4, as said below
Outputs:
- correlations: float32 [8, 16, 4, 128, 256], P('win', 'chan')
The draws below stay inside these ranges and needn't reach their ends.
Inputs may be any that keep to these rules, and one draw needn't show every extreme that they name: `pair_remote`: for owner block b, slots below pair_count[b] list distinct blocks r != b with |r - b| <= 2 in rising order; the other slots hold 0. `pair_count`: some owner block lists all 4 pairs.
All inputs are finite; a program needn't handle non-finite values.
Results may differ from the reference program's by a relative error of at most 0.0049.
Values may be sent and summed in bfloat16 or wider, within the bound.
No kernel may reach another device: no remote copies, remote signals or barrier semaphores. Data moves between devices by JAX's collectives and lax.ppermute only.
A program may use at most 64 MiB of HBM per device.

```python
import math
import jax
import jax.numpy as jnp
from jax import lax

CH = 128
BINS = 4096
BAND = 64
LAGS = 256
V = 8
REACH = 2
MAXP = 4
WINDOWS = 8
BLOCKS = 16
CHANNELS = 2048


def pair_table(key):
    key = jax.random.fold_in(key, 5)
    mask_key, full_key = jax.random.split(key)
    owner = jnp.arange(BLOCKS, dtype=jnp.int32)[:, None]
    offsets = jnp.concatenate([jnp.arange(-REACH, 0, dtype=jnp.int32), jnp.arange(1, REACH + 1, dtype=jnp.int32)])
    candidate = owner + offsets[None, :]
    inside = (candidate >= 0) & (candidate < BLOCKS)
    keep = jax.random.randint(mask_key, (BLOCKS, MAXP), 0, 4) > 0
    full_owner = jax.random.randint(full_key, (), REACH, BLOCKS - REACH)
    keep = keep | (owner == full_owner)
    keep = keep | (owner == BLOCKS - 2) & (offsets[None, :] == 1)
    valid = inside & keep
    slots = jnp.arange(MAXP, dtype=jnp.int32)
    order_key = jnp.where(valid, 0, MAXP).astype(jnp.int32) + slots[None, :]
    order = jnp.argsort(order_key, axis=1)
    remote = jnp.take_along_axis(candidate, order, axis=1)
    listed = jnp.sum(valid.astype(jnp.int32), axis=1)
    remote = jnp.where(slots[None, :] < listed[:, None], remote, 0)
    return (remote.astype(jnp.int32), listed.astype(jnp.int32))


def draw_pair_remote(key, part):
    return pair_table(key)[0]


def draw_pair_count(key, part):
    return pair_table(key)[1]


def draw_spectra(key, part):
    key = jax.random.fold_in(key, 11)
    band_key, rough_key, base_key = jax.random.split(key, 3)
    band_count = BINS // BAND
    full = (WINDOWS, CHANNELS, 2, band_count, BAND)
    rough = jax.random.uniform(rough_key, full, jnp.float32, 0.5, 2.0)
    band_scale = jnp.exp(jax.random.uniform(band_key, (WINDOWS, CHANNELS, 1, band_count, 1), jnp.float32) * math.log(10.0))
    values = jax.random.normal(base_key, full, jnp.float32)
    result = jnp.clip(values * band_scale * rough, -40.0, 40.0)
    return result.reshape(WINDOWS, CHANNELS, 2 * BINS).astype(jnp.bfloat16)


def setup_inputs(seed: int = 0) -> dict:
    key_of = jax.random.split(jax.random.key(seed), 4)
    return {
        "spectra": draw_spectra(jax.random.fold_in(key_of[3], 71), 0),
        "pair_remote": draw_pair_remote(jax.random.fold_in(key_of[3], 71), 0),
        "pair_count": draw_pair_count(jax.random.fold_in(key_of[3], 71), 0),
    }


def whiten(spectra):
    values = spectra.astype(jnp.float32)
    bin_count = values.shape[-1] // 2
    real_part = values[..., :bin_count]
    imag_part = values[..., bin_count:]
    magnitude = jnp.sqrt(real_part * real_part + imag_part * imag_part)
    shape = magnitude.shape[:-1] + (bin_count // BAND, BAND)
    level = lax.optimization_barrier(jnp.mean(magnitude.reshape(shape), axis=-1, keepdims=True)) + 1e-06
    level = jnp.broadcast_to(level, shape).reshape(magnitude.shape)
    return jnp.concatenate([real_part / level, imag_part / level], axis=-1).astype(jnp.bfloat16)

def phase_tables(bin_count):
    lag_index = jnp.arange(LAGS, dtype=jnp.int32) - LAGS // 2
    freq_index = jnp.arange(bin_count, dtype=jnp.int32)
    phase = lag_index[:, None] * freq_index[None, :] % (2 * bin_count)
    angle = phase.astype(jnp.float32) * (math.pi / bin_count)
    return (jnp.cos(angle), jnp.sin(angle))

def rotate(source, cos_table, sin_table):
    bin_count = source.shape[-1] // 2
    real_part = source[..., None, :bin_count]
    imag_part = source[..., None, bin_count:]
    rot_real = real_part * cos_table - imag_part * sin_table
    rot_imag = real_part * sin_table + imag_part * cos_table
    return jnp.concatenate([rot_real, rot_imag], axis=-1).astype(jnp.bfloat16)

def reference(spectra, pair_remote, pair_count):
    whitened = whiten(spectra)
    bin_count = BINS
    cos_table, sin_table = phase_tables(bin_count)
    stride = CH // V
    scale = 1.0 / math.sqrt(BINS * WINDOWS)

    def one_owner(owner):
        block = lax.dynamic_slice_in_dim(whitened, owner * CH, CH, 1)
        source = block[:, ::stride].astype(jnp.float32)
        remotes = pair_remote[owner]

        def take_block(remote):
            return lax.dynamic_slice_in_dim(whitened, remote * CH, CH, 1)
        gathered = lax.map(take_block, remotes)

        def one_source(index):
            picked = lax.dynamic_slice_in_dim(source, index, 1, 1)[:, 0]
            rotated = rotate(picked, cos_table, sin_table)
            left = rotated.transpose(1, 0, 2).reshape(LAGS, -1)
            right = gathered.transpose(1, 3, 0, 2).reshape(left.shape[1], -1)
            result = jnp.dot(left, right, preferred_element_type=jnp.float32)
            return result.reshape(LAGS, MAXP, CH).transpose(1, 2, 0) * scale
        corr = lax.map(one_source, jnp.arange(V, dtype=jnp.int32))
        live = jnp.arange(MAXP, dtype=jnp.int32) < pair_count[owner]
        return jnp.where(live[None, :, None, None], corr, jnp.float32(0.0))
    result = lax.map(one_owner, jnp.arange(BLOCKS, dtype=jnp.int32))
    return jnp.transpose(result, (1, 0, 2, 3, 4))
```

```python
import functools
import math

import jax
import jax.numpy as jnp
import ml_dtypes
import numpy as np
from jax import lax
from jax.experimental import pallas as pl
from jax.experimental.pallas import tpu as pltpu
from jax.sharding import PartitionSpec as P

BAND = 64
LAGS = 256
REACH = 2
CHUNK = 1024
VMEM = 48 * 1024 * 1024
OFFSETS = (-2, -1, 1, 2)


def lag_table(bins):
    t = np.arange(LAGS) - LAGS // 2
    f = np.arange(bins)
    angle = ((f[:, None] * t[None, :]) % (2 * bins)) * (math.pi / bins)
    table = np.concatenate([np.cos(angle), -np.sin(angle)], axis=0)
    return table.astype(np.float32).astype(ml_dtypes.bfloat16)


def band_matrix():
    band = np.arange(128) // BAND
    return (band[:, None] == band[None, :]).astype(ml_dtypes.bfloat16)


def whiten_rows(values, ones):
    rows, width = values.shape
    bins = width // 2
    real, imag = values[:, :bins], values[:, bins:]
    magnitude = jnp.sqrt(real * real + imag * imag)
    parts = bins // 128
    stacked = jnp.concatenate([magnitude[:, i * 128 : (i + 1) * 128] for i in range(parts)], axis=0)
    high = stacked.astype(jnp.bfloat16)
    low = (stacked - high.astype(jnp.float32)).astype(jnp.bfloat16)
    total = jnp.dot(high, ones, preferred_element_type=jnp.float32) + jnp.dot(
        low, ones, preferred_element_type=jnp.float32
    )
    inverse = 1.0 / (total * (1.0 / BAND) + 1e-06)
    inverse = jnp.concatenate([inverse[i * rows : (i + 1) * rows] for i in range(parts)], axis=1)
    return jnp.concatenate([real * inverse, imag * inverse], axis=1).astype(jnp.bfloat16)


def source_kernel(spectra, ones, out):
    rows = [spectra[w].astype(jnp.float32)[0:1] for w in range(spectra.shape[0])]
    out[...] = whiten_rows(jnp.concatenate(rows, axis=0), ones[...])


def whiten_kernel(spectra, ones, out):
    out[0] = whiten_rows(spectra[0].astype(jnp.float32), ones[...])


def whiten_source(spectra, ones):
    windows, _, width = spectra.shape
    return pl.pallas_call(
        source_kernel,
        out_shape=jax.ShapeDtypeStruct((windows, width), jnp.bfloat16),
        compiler_params=pltpu.CompilerParams(vmem_limit_bytes=VMEM),
        cost_estimate=pl.CostEstimate(flops=10**6, bytes_accessed=2 * 2**20, transcendentals=0),
        name="whiten_source",
    )(spectra, ones)


def whiten_all(spectra, ones):
    windows, channels, width = spectra.shape
    block = pl.BlockSpec((1, channels, width), lambda w: (w, 0, 0))
    return pl.pallas_call(
        whiten_kernel,
        grid=(windows,),
        in_specs=[block, pl.BlockSpec(ones.shape, lambda w: (0, 0))],
        out_specs=block,
        out_shape=jax.ShapeDtypeStruct(spectra.shape, jnp.bfloat16),
        compiler_params=pltpu.CompilerParams(vmem_limit_bytes=VMEM),
        cost_estimate=pl.CostEstimate(flops=10**7, bytes_accessed=4 * 2**20, transcendentals=0),
        name="whiten_all",
    )(spectra, ones)


def tree(terms):
    while len(terms) > 1:
        terms = [terms[i] + terms[i + 1] for i in range(0, len(terms), 2)]
    return terms[0]


def correlate_kernel(groups, scale, parity, *refs):
    own_r, own_i, sib_r, sib_i = refs[:4]
    sources = [(refs[4 + 2 * g], refs[5 + 2 * g]) for g in range(groups)]
    cos, sin, out, acc, prod_r, prod_i, src_r, src_i, src_s = refs[4 + 2 * groups :]
    step = pl.program_id(0)
    windows, half = own_r.shape[0], own_r.shape[1]
    per, chunk = sources[0][0].shape[0], own_r.shape[2]
    for g, (re, im) in enumerate(sources):
        rows = slice(g * per, (g + 1) * per)
        a, b = re[...].astype(jnp.float32), im[...].astype(jnp.float32)
        src_r[rows] = a
        src_i[rows] = b
        src_s[rows] = a + b

    @pl.when(step == 0)
    def _():
        acc[...] = jnp.zeros_like(acc)

    def body(q, carry):
        lanes = pl.ds(pl.multiple_of(q * 128, 128), 128)
        for h, (xr, xi) in enumerate(((own_r, own_i), (sib_r, sib_i))):
            first = pl.multiple_of((parity[0] + h) % 2 * half, half)
            re = [xr[w, :, lanes].astype(jnp.float32) for w in range(windows)]
            im = [xi[w, :, lanes].astype(jnp.float32) for w in range(windows)]
            for s in range(groups * per):
                parts_r, parts_i = [], []
                for t in range(0, half, 8):
                    one, two, three = [], [], []
                    for w in range(windows):
                        x, y = re[w][t : t + 8], im[w][t : t + 8]
                        wide = x.shape
                        one.append(jnp.broadcast_to(src_s[s, w : w + 1, lanes], wide) * x)
                        two.append(jnp.broadcast_to(src_r[s, w : w + 1, lanes], wide) * (x + y))
                        three.append(jnp.broadcast_to(src_i[s, w : w + 1, lanes], wide) * (x - y))
                    base = tree(one)
                    parts_r.append(base - tree(three))
                    parts_i.append(base - tree(two))
                rows = pl.ds(s * 2 * half + first, half)
                prod_r[rows, lanes] = jnp.concatenate(parts_r, axis=0).astype(jnp.bfloat16)
                prod_i[rows, lanes] = jnp.concatenate(parts_i, axis=0).astype(jnp.bfloat16)
        return carry

    lax.fori_loop(0, chunk // 128, body, 0)
    acc[...] += jnp.dot(prod_r[...], cos[...], preferred_element_type=jnp.float32) + jnp.dot(
        prod_i[...], sin[...], preferred_element_type=jnp.float32
    )

    @pl.when(step == pl.num_programs(0) - 1)
    def _():
        out[...] = (acc[...] * scale).reshape(out.shape).astype(out.dtype)


def correlate(parity, own, sibling, sources, table, scale):
    windows, half, width = own.shape
    bins = width // 2
    steps = bins // CHUNK
    groups, per = len(sources), sources[0].shape[0]
    n = groups * per

    def pair(shape):
        lead = (0,) * (len(shape) - 1)
        return [
            pl.BlockSpec(shape, lambda j, lead=lead: lead + (j,)),
            pl.BlockSpec(shape, lambda j, lead=lead: lead + (steps + j,)),
        ]

    x_spec, s_spec = pair((windows, half, CHUNK)), pair((per, windows, CHUNK))
    out_shape = (n, 2 * half, LAGS)
    return pl.pallas_call(
        functools.partial(correlate_kernel, groups, scale),
        grid=(steps,),
        in_specs=[pl.BlockSpec(memory_space=pltpu.SMEM)]
        + x_spec * 2
        + s_spec * groups
        + [
            pl.BlockSpec((CHUNK, LAGS), lambda j: (j, 0)),
            pl.BlockSpec((CHUNK, LAGS), lambda j: (steps + j, 0)),
        ],
        out_specs=pl.BlockSpec(out_shape, lambda j: (0, 0, 0)),
        out_shape=jax.ShapeDtypeStruct(out_shape, jnp.bfloat16),
        scratch_shapes=[
            pltpu.VMEM((n * 2 * half, LAGS), jnp.float32),
            pltpu.VMEM((n * 2 * half, CHUNK), jnp.bfloat16),
            pltpu.VMEM((n * 2 * half, CHUNK), jnp.bfloat16),
            pltpu.VMEM((n, windows, CHUNK), jnp.float32),
            pltpu.VMEM((n, windows, CHUNK), jnp.float32),
            pltpu.VMEM((n, windows, CHUNK), jnp.float32),
        ],
        compiler_params=pltpu.CompilerParams(vmem_limit_bytes=VMEM),
        cost_estimate=pl.CostEstimate(
            flops=n * 10**9, bytes_accessed=8 * 2**20, transcendentals=0
        ),
        name=f"correlate_{n}",
    )(parity, own, own, sibling, sibling, *[s for s in sources for _ in range(2)], table, table)


def chan_shift(block, distance):
    size = lax.axis_size("chan")
    return lax.ppermute(block, "chan", [(i, (i + distance) % size) for i in range(size)])


def chip_shift(block, distance):
    size = lax.axis_size("win")
    return lax.ppermute(block, "win", [(i, (i + 2 * distance) % size) for i in range(size)])


def core_swap(block):
    size = lax.axis_size("win")
    return lax.ppermute(block, "win", [(i, i ^ 1) for i in range(size)])


def on_device(spectra, pair_remote, pair_count):
    windows, channels, width = spectra.shape
    bins = width // 2
    scale = 1.0 / math.sqrt(bins * windows)
    ones = jnp.asarray(band_matrix())
    table = jnp.asarray(lag_table(bins))
    parity = (lax.axis_index("win") % 2).astype(jnp.int32)[None]

    source = whiten_source(spectra, ones)
    near = jnp.stack([chan_shift(source, d) for d in OFFSETS])
    own = whiten_all(spectra, ones)
    sibling = core_swap(own)
    up, down, far = chip_shift(near, 1), chip_shift(near, -1), chip_shift(near, 2)

    args = (table, scale)
    c_own = correlate(parity, own, sibling, [near], *args)
    c_two = correlate(parity, own, sibling, [up, down], *args)
    c_far = correlate(parity, own, sibling, [far], *args)
    c_up, c_down = c_two[: len(OFFSETS)], c_two[len(OFFSETS) :]

    chips = lax.axis_size("win") // 2
    chip = lax.axis_index("win") // 2
    home = [c_own, chip_shift(c_down, 1), chip_shift(c_far, 2), chip_shift(c_up, -1)]
    stacked = jnp.stack(home)
    order = (chip - jnp.arange(chips)) % chips
    stacked = stacked[order]
    blocks = jnp.swapaxes(stacked, 0, 1).reshape(len(OFFSETS), chips * 2 * channels, LAGS)
    back = [chan_shift(blocks[i], -d) for i, d in enumerate(OFFSETS)]

    distance = pair_remote[0] - lax.axis_index("chan")
    live = jnp.arange(pair_remote.shape[1], dtype=jnp.int32) < pair_count[0]
    result = jnp.zeros((pair_remote.shape[1],) + back[0].shape, jnp.float32)
    for block, d in zip(back, OFFSETS):
        chosen = (live & (distance == d))[:, None, None]
        result = jnp.where(chosen, block[None].astype(jnp.float32), result)
    return result[None, None]


def solution(mesh):
    in_specs = (P(None, ("chan", "win"), None), P("chan", None), P("chan"))
    out_specs = P("win", "chan", None, None, None)
    return jax.shard_map(
        on_device, mesh=mesh, in_specs=in_specs, out_specs=out_specs, check_vma=False
    )
```

```python
import functools
import math

import jax
import jax.numpy as jnp
import ml_dtypes
import numpy as np
from jax import lax
from jax.experimental import pallas as pl
from jax.experimental.pallas import tpu as pltpu
from jax.sharding import PartitionSpec as P

BAND = 64
LAGS = 256
REACH = 2
VMEM = 24 * 1024 * 1024
OFFSETS = (-2, -1, 1, 2)


def lag_table(bins):
    t = np.arange(LAGS) - LAGS // 2
    f = np.arange(bins)
    angle = ((f[:, None] * t[None, :]) % (2 * bins)) * (math.pi / bins)
    table = np.concatenate([np.cos(angle), -np.sin(angle)], axis=0)
    return table.astype(np.float32).astype(ml_dtypes.bfloat16)


def band_matrix():
    row = lax.broadcasted_iota(jnp.int32, (128, 128), 0) // BAND
    column = lax.broadcasted_iota(jnp.int32, (128, 128), 1) // BAND
    return jnp.where(row == column, 1.0, 0.0).astype(jnp.bfloat16)


def whiten_rows(values):
    ones = band_matrix()
    rows, width = values.shape
    bins = width // 2
    real, imag = values[:, :bins], values[:, bins:]
    magnitude = jnp.sqrt(real * real + imag * imag)
    parts = bins // 128
    stacked = jnp.concatenate([magnitude[:, i * 128 : (i + 1) * 128] for i in range(parts)], axis=0)
    high = stacked.astype(jnp.bfloat16)
    low = (stacked - high.astype(jnp.float32)).astype(jnp.bfloat16)
    total = jnp.dot(high, ones, preferred_element_type=jnp.float32) + jnp.dot(
        low, ones, preferred_element_type=jnp.float32
    )
    inverse = 1.0 / (total * (1.0 / BAND) + 1e-06)
    inverse = jnp.concatenate([inverse[i * rows : (i + 1) * rows] for i in range(parts)], axis=1)
    return jnp.concatenate([real * inverse, imag * inverse], axis=1).astype(jnp.bfloat16)


def source_kernel(spectra, out):
    rows = [spectra[w].astype(jnp.float32)[0:1] for w in range(spectra.shape[0])]
    out[...] = whiten_rows(jnp.concatenate(rows, axis=0))


def whiten_kernel(own, sibling, own_out, sibling_out):
    own_out[0] = whiten_rows(own[0].astype(jnp.float32))
    sibling_out[0] = whiten_rows(sibling[0].astype(jnp.float32))


def whiten_source(spectra):
    windows, _, width = spectra.shape
    return pl.pallas_call(
        source_kernel,
        out_shape=jax.ShapeDtypeStruct((windows, width), jnp.bfloat16),
        compiler_params=pltpu.CompilerParams(vmem_limit_bytes=VMEM),
        cost_estimate=pl.CostEstimate(flops=10**6, bytes_accessed=2 * 2**20, transcendentals=0),
        name="whiten_source",
    )(spectra)


def whiten_both(own, sibling):
    windows, channels, width = own.shape
    block = pl.BlockSpec((1, channels, width), lambda w: (w, 0, 0))
    shape = jax.ShapeDtypeStruct(own.shape, jnp.bfloat16)
    return pl.pallas_call(
        whiten_kernel,
        grid=(windows,),
        in_specs=[block, block],
        out_specs=[block, block],
        out_shape=[shape, shape],
        compiler_params=pltpu.CompilerParams(vmem_limit_bytes=VMEM),
        cost_estimate=pl.CostEstimate(flops=10**9, bytes_accessed=8 * 2**20, transcendentals=0),
        name="whiten_both",
    )(own, sibling)


def correlate_kernel(groups, scale, parity, *refs):
    own, sib = refs[:2]
    sources = refs[2 : 2 + groups]
    table_hbm, out, prod_r, prod_i, src_r, src_i, src_s, table, done = refs[2 + groups :]
    fetch = pltpu.make_async_copy(table_hbm, table, done)
    fetch.start()
    windows, half, width = own.shape
    bins = width // 2
    per = sources[0].shape[0]
    for g, ref in enumerate(sources):
        rows = slice(g * per, (g + 1) * per)
        a, b = ref[:, :, :bins].astype(jnp.float32), ref[:, :, bins:].astype(jnp.float32)
        src_r[rows] = a
        src_i[rows] = b
        src_s[rows] = a + b

    def body(q, carry):
        lanes = pl.ds(pl.multiple_of(q * 128, 128), 128)
        upper = pl.ds(pl.multiple_of(bins + q * 128, 128), 128)
        for h, ref in enumerate((own, sib)):
            place = (parity[0] + h) % 2
            for t in range(0, half, 8):
                chan = []
                for w in range(windows):
                    x = ref[w, :, lanes].astype(jnp.float32)[t : t + 8]
                    y = ref[w, :, upper].astype(jnp.float32)[t : t + 8]
                    chan.append((x, x + y, x - y))
                for s in range(groups * per):
                    total = None
                    for w in range(windows):
                        terms = [
                            jnp.broadcast_to(r[s, w : w + 1, lanes], (8, 128)) * c
                            for r, c in zip((src_s, src_r, src_i), chan[w])
                        ]
                        total = terms if total is None else [p + q for p, q in zip(total, terms)]
                    tile = (s * 2 + place) * (half // 8) + t // 8
                    prod_r[tile, :, lanes] = (total[0] - total[2]).astype(jnp.bfloat16)
                    prod_i[tile, :, lanes] = (total[0] - total[1]).astype(jnp.bfloat16)
        return carry

    def rows(ref):
        return ref[...].reshape(ref.shape[0] * 8, bins)

    lax.fori_loop(0, bins // 128, body, 0)
    fetch.wait()
    total = jnp.dot(rows(prod_r), table[:bins], preferred_element_type=jnp.float32) + jnp.dot(
        rows(prod_i), table[bins:], preferred_element_type=jnp.float32
    )
    out[...] = (total * scale).reshape(out.shape).astype(out.dtype)


def correlate(parity, own, sibling, sources, table, scale):
    windows, half, width = own.shape
    bins = width // 2
    groups, per = len(sources), sources[0].shape[0]
    n = groups * per
    whole = pl.BlockSpec(memory_space=pltpu.VMEM)
    return pl.pallas_call(
        functools.partial(correlate_kernel, groups, scale),
        in_specs=[pl.BlockSpec(memory_space=pltpu.SMEM)] + [whole] * (2 + groups)
        + [pl.BlockSpec(memory_space=pl.ANY)],
        out_specs=whole,
        out_shape=jax.ShapeDtypeStruct((n, 2 * half, LAGS), jnp.bfloat16),
        scratch_shapes=[
            pltpu.VMEM((n * 2 * half // 8, 8, bins), jnp.bfloat16),
            pltpu.VMEM((n * 2 * half // 8, 8, bins), jnp.bfloat16),
            pltpu.VMEM((n, windows, bins), jnp.float32),
            pltpu.VMEM((n, windows, bins), jnp.float32),
            pltpu.VMEM((n, windows, bins), jnp.float32),
            pltpu.VMEM(table.shape, table.dtype),
            pltpu.SemaphoreType.DMA,
        ],
        compiler_params=pltpu.CompilerParams(vmem_limit_bytes=VMEM),
        cost_estimate=pl.CostEstimate(
            flops=n * 10**9, bytes_accessed=8 * 2**20, transcendentals=0
        ),
        name=f"correlate_{n}",
    )(parity, own, sibling, *sources, table)


def chan_shift(block, distance):
    size = lax.axis_size("chan")
    return lax.ppermute(block, "chan", [(i, (i + distance) % size) for i in range(size)])


def chip_shift(block, distance):
    size = lax.axis_size("win")
    return lax.ppermute(block, "win", [(i, (i + 2 * distance) % size) for i in range(size)])


def core_swap(block):
    size = lax.axis_size("win")
    return lax.ppermute(block, "win", [(i, i ^ 1) for i in range(size)])


def on_device(spectra, pair_remote, pair_count):
    windows, channels, width = spectra.shape
    bins = width // 2
    scale = 1.0 / math.sqrt(bins * windows)
    table = jnp.asarray(lag_table(bins))
    parity = (lax.axis_index("win") % 2).astype(jnp.int32)[None]

    other = core_swap(spectra)
    source = whiten_source(spectra)
    near = jnp.stack([chan_shift(source, d) for d in OFFSETS])
    own, sibling = whiten_both(spectra, other)

    args = (table, scale)
    up, down = chip_shift(near, 1), chip_shift(near, -1)
    part = len(OFFSETS) // 2
    c_first = correlate(parity, own, sibling, [near[:part]], *args)
    near, c_first = lax.optimization_barrier((near, c_first))
    far = chip_shift(near, 2)
    c_two = correlate(parity, own, sibling, [up, down], *args)
    c_up, c_down = c_two[: len(OFFSETS)], c_two[len(OFFSETS) :]
    far, c_up, c_down = lax.optimization_barrier((far, c_up, c_down))
    c_far = correlate(parity, own, sibling, [far], *args)
    last, c_far = lax.optimization_barrier((near[part:], c_far))
    c_own = jnp.concatenate([c_first, correlate(parity, own, sibling, [last], *args)])

    chips = lax.axis_size("win") // 2
    chip = lax.axis_index("win") // 2
    home = [c_own, chip_shift(c_down, 1), chip_shift(c_far, 2), chip_shift(c_up, -1)]
    stacked = jnp.stack(home)
    order = (chip - jnp.arange(chips)) % chips
    stacked = stacked[order]
    blocks = jnp.swapaxes(stacked, 0, 1).reshape(len(OFFSETS), chips * 2 * channels, LAGS)
    back = [chan_shift(blocks[i], -d) for i, d in enumerate(OFFSETS)]

    distance = pair_remote[0] - lax.axis_index("chan")
    live = jnp.arange(pair_remote.shape[1], dtype=jnp.int32) < pair_count[0]
    result = jnp.zeros((pair_remote.shape[1],) + back[0].shape, jnp.float32)
    for block, d in zip(back, OFFSETS):
        chosen = (live & (distance == d))[:, None, None]
        result = jnp.where(chosen, block[None].astype(jnp.float32), result)
    return result[None, None]


def solution(mesh):
    in_specs = (P(None, ("chan", "win"), None), P("chan", None), P("chan"))
    out_specs = P("win", "chan", None, None, None)
    return jax.shard_map(
        on_device, mesh=mesh, in_specs=in_specs, out_specs=out_specs, check_vma=False
    )
```

```python
import functools
import math

import jax
import jax.numpy as jnp
import ml_dtypes
import numpy as np
from jax import lax
from jax.experimental import pallas as pl
from jax.experimental.pallas import tpu as pltpu
from jax.sharding import PartitionSpec as P

BAND = 64
LAGS = 256
REACH = 2
VMEM = 12 * 2**20
WIDE = 48 * 2**20
ROUTES = 4


def lag_table(bins):
    t = np.arange(LAGS) - LAGS // 2
    f = np.arange(bins)
    angle = ((f[:, None] * t[None, :]) % (2 * bins)) * (math.pi / bins)
    table = np.concatenate([np.cos(angle), -np.sin(angle)], axis=0)
    return table.astype(np.float32).astype(ml_dtypes.bfloat16)


def band_matrix():
    row = lax.broadcasted_iota(jnp.int32, (128, 128), 0) // BAND
    column = lax.broadcasted_iota(jnp.int32, (128, 128), 1) // BAND
    return jnp.where(row == column, 1.0, 0.0).astype(jnp.bfloat16)


def whiten_rows(values):
    ones = band_matrix()
    rows, width = values.shape
    bins = width // 2
    real, imag = values[:, :bins], values[:, bins:]
    magnitude = jnp.sqrt(real * real + imag * imag)
    parts = bins // 128
    stacked = jnp.concatenate([magnitude[:, i * 128 : (i + 1) * 128] for i in range(parts)], axis=0)
    high = stacked.astype(jnp.bfloat16)
    low = (stacked - high.astype(jnp.float32)).astype(jnp.bfloat16)
    total = jnp.dot(high, ones, preferred_element_type=jnp.float32) + jnp.dot(
        low, ones, preferred_element_type=jnp.float32
    )
    inverse = 1.0 / (total * (1.0 / BAND) + 1e-06)
    inverse = jnp.concatenate([inverse[i * rows : (i + 1) * rows] for i in range(parts)], axis=1)
    return jnp.concatenate([real * inverse, imag * inverse], axis=1).astype(jnp.bfloat16)


def source_kernel(spectra, out):
    rows = [spectra[w].astype(jnp.float32)[0:1] for w in range(spectra.shape[0])]
    out[...] = whiten_rows(jnp.concatenate(rows, axis=0))


def whiten_kernel(flag, own, sibling, own_out, sibling_out, flag_out, held, done):
    windows = own.shape[0]
    pairs = ((own, own_out), (sibling, sibling_out))
    copies = [
        pltpu.make_async_copy(pairs[k][0].at[w], held.at[k, w], done.at[k, w])
        for w in range(windows)
        for k in range(2)
    ]
    for copy in copies:
        copy.start()
    for i, copy in enumerate(copies):
        w, k = i // 2, i % 2
        copy.wait()
        pairs[k][1][w] = whiten_rows(held[k, w].astype(jnp.float32))
    flag_out[0] = flag[0]


def whiten_source(spectra):
    windows, _, width = spectra.shape
    return pl.pallas_call(
        source_kernel,
        out_shape=jax.ShapeDtypeStruct((windows, width), jnp.bfloat16),
        compiler_params=pltpu.CompilerParams(vmem_limit_bytes=VMEM),
        cost_estimate=pl.CostEstimate(flops=10**6, bytes_accessed=2 * 2**20, transcendentals=0),
        name="whiten_source",
    )(spectra)


def whiten_both(own, sibling, flag):
    windows = own.shape[0]
    shape = jax.ShapeDtypeStruct(own.shape, jnp.bfloat16)
    scalar, whole = pl.BlockSpec(memory_space=pltpu.SMEM), pl.BlockSpec(memory_space=pltpu.VMEM)
    return pl.pallas_call(
        whiten_kernel,
        in_specs=[scalar] + [pl.BlockSpec(memory_space=pltpu.HBM)] * 2,
        out_specs=[whole, whole, scalar],
        out_shape=[shape, shape, jax.ShapeDtypeStruct(flag.shape, flag.dtype)],
        scratch_shapes=[
            pltpu.VMEM((2,) + own.shape, own.dtype),
            pltpu.SemaphoreType.DMA((2, windows)),
        ],
        compiler_params=pltpu.CompilerParams(vmem_limit_bytes=VMEM),
        cost_estimate=pl.CostEstimate(flops=10**9, bytes_accessed=8 * 2**20, transcendentals=0),
        name="whiten_both",
    )(flag, own, sibling)


def correlate_kernel(groups, scale, parity, *refs):
    own, sib = refs[:2]
    sources = refs[2 : 2 + groups]
    table_hbm, out, prod_r, prod_i, src_r, src_i, src_s, table, done = refs[2 + groups :]
    fetch = pltpu.make_async_copy(table_hbm, table, done)
    fetch.start()
    windows, half, width = own.shape
    bins = width // 2
    per = sources[0].shape[0]
    for g, ref in enumerate(sources):
        rows = slice(g * per, (g + 1) * per)
        a, b = ref[:, :, :bins].astype(jnp.float32), ref[:, :, bins:].astype(jnp.float32)
        src_r[rows] = a
        src_i[rows] = b
        src_s[rows] = a + b

    def body(q, carry):
        lanes = pl.ds(pl.multiple_of(q * 128, 128), 128)
        upper = pl.ds(pl.multiple_of(bins + q * 128, 128), 128)
        for h, ref in enumerate((own, sib)):
            place = (parity[0] + h) % 2
            for t in range(0, half, 8):
                chan = []
                for w in range(windows):
                    x = ref[w, :, lanes].astype(jnp.float32)[t : t + 8]
                    y = ref[w, :, upper].astype(jnp.float32)[t : t + 8]
                    chan.append((x, x + y, x - y))
                for s in range(groups * per):
                    total = None
                    for w in range(windows):
                        terms = [
                            jnp.broadcast_to(r[s, w : w + 1, lanes], (8, 128)) * c
                            for r, c in zip((src_s, src_r, src_i), chan[w])
                        ]
                        total = terms if total is None else [p + q for p, q in zip(total, terms)]
                    tile = (s * 2 + place) * (half // 8) + t // 8
                    prod_r[tile, :, lanes] = (total[0] - total[2]).astype(jnp.bfloat16)
                    prod_i[tile, :, lanes] = (total[0] - total[1]).astype(jnp.bfloat16)
        return carry

    def rows(ref):
        return ref[...].reshape(ref.shape[0] * 8, bins)

    lax.fori_loop(0, bins // 128, body, 0)
    fetch.wait()
    total = jnp.dot(rows(prod_r), table[:bins], preferred_element_type=jnp.float32) + jnp.dot(
        rows(prod_i), table[bins:], preferred_element_type=jnp.float32
    )
    out[...] = (total * scale).reshape(out.shape).astype(out.dtype)


def correlate(parity, own, sibling, sources, table, scale):
    windows, half, width = own.shape
    bins = width // 2
    groups, per = len(sources), sources[0].shape[0]
    n = groups * per
    whole = pl.BlockSpec(memory_space=pltpu.VMEM)
    return pl.pallas_call(
        functools.partial(correlate_kernel, groups, scale),
        in_specs=[pl.BlockSpec(memory_space=pltpu.SMEM)] + [whole] * (2 + groups)
        + [pl.BlockSpec(memory_space=pltpu.HBM)],
        out_specs=whole,
        out_shape=jax.ShapeDtypeStruct((n, 2 * half, LAGS), jnp.bfloat16),
        scratch_shapes=[
            pltpu.VMEM((n * 2 * half // 8, 8, bins), jnp.bfloat16),
            pltpu.VMEM((n * 2 * half // 8, 8, bins), jnp.bfloat16),
            pltpu.VMEM((n, windows, bins), jnp.float32),
            pltpu.VMEM((n, windows, bins), jnp.float32),
            pltpu.VMEM((n, windows, bins), jnp.float32),
            pltpu.VMEM(table.shape, table.dtype),
            pltpu.SemaphoreType.DMA,
        ],
        compiler_params=pltpu.CompilerParams(vmem_limit_bytes=WIDE),
        cost_estimate=pl.CostEstimate(
            flops=n * 10**9, bytes_accessed=8 * 2**20, transcendentals=0
        ),
        name=f"correlate_{n}",
    )(parity, own, sibling, *sources, table)


def routes(blocks):
    cycle = [min(b + 2, blocks - 1) if b % 2 == 0 else max(b - 2, 0) for b in range(blocks)]
    inverse = [cycle.index(b) for b in range(blocks)]
    up = [(b + 1) % blocks for b in range(blocks)]
    down = [(b - 1) % blocks for b in range(blocks)]
    return cycle, up, down, inverse


def targets(block, blocks):
    odd, last = block % 2 == 1, blocks - 1
    cycle = jnp.where(odd, jnp.maximum(block - 2, 0), jnp.minimum(block + 2, last))
    above = jnp.where(block == last, last - 1, block + 2)
    below = jnp.where(block == 0, 1, block - 2)
    return cycle, block + 1, block - 1, jnp.where(odd, above, below)


def route_swap(block, index, back=False):
    pairs = enumerate(routes(lax.axis_size("chan"))[index])
    return lax.ppermute(block, "chan", [(j, i) if back else (i, j) for i, j in pairs])


def chip_shift(block, distance):
    size = lax.axis_size("win")
    return lax.ppermute(block, "win", [(i, (i + 2 * distance) % size) for i in range(size)])


def core_swap(block):
    size = lax.axis_size("win")
    return lax.ppermute(block, "win", [(i, i ^ 1) for i in range(size)])


def on_device(spectra, pair_remote, pair_count):
    windows, channels, width = spectra.shape
    bins = width // 2
    scale = 1.0 / math.sqrt(bins * windows)
    table = jnp.asarray(lag_table(bins))
    parity = (lax.axis_index("win") % 2).astype(jnp.int32)[None]

    other = core_swap(spectra)
    source = whiten_source(spectra)
    arrived = [route_swap(source, i) for i in range(ROUTES)]
    own, sibling, pair_count = whiten_both(spectra, other, pair_count)
    arrived, pair_count = lax.optimization_barrier((arrived, pair_count))
    half = ROUTES // 2
    first, second = jnp.stack(arrived[:half]), jnp.stack(arrived[half:])

    up_first, down_first = chip_shift(first, 1), chip_shift(first, -1)
    up_second, down_second = chip_shift(second, 1), chip_shift(second, -1)
    run = functools.partial(correlate, parity, own, sibling, table=table, scale=scale)
    own_first = run([first])
    own_first, up_first, down_first = lax.optimization_barrier((own_first, up_first, down_first))
    far_first = chip_shift(up_first, 1)
    near_first = run([up_first, down_first])
    near_first, up_second, down_second = lax.optimization_barrier(
        (near_first, up_second, down_second)
    )
    far_second = chip_shift(down_second, -1)
    near_second = run([up_second, down_second])
    near_second, far_first, far_second = lax.optimization_barrier(
        (near_second, far_first, far_second)
    )
    c_far = run([far_first, far_second])
    c_far, second = lax.optimization_barrier((c_far, second))
    c_own = jnp.concatenate([own_first, run([second])])
    c_up = jnp.concatenate([near_first[:half], near_second[:half]])
    c_down = jnp.concatenate([near_first[half:], near_second[half:]])

    chips = lax.axis_size("win") // 2
    chip = lax.axis_index("win") // 2
    home = [c_own, chip_shift(c_down, 1), chip_shift(c_far, 2), chip_shift(c_up, -1)]
    stacked = jnp.stack(home)
    order = (chip - jnp.arange(chips)) % chips
    stacked = stacked[order]
    blocks = jnp.swapaxes(stacked, 0, 1).reshape(ROUTES, chips * 2 * channels, LAGS)
    back = [route_swap(blocks[i], i, back=True) for i in range(ROUTES)]

    met = targets(lax.axis_index("chan"), lax.axis_size("chan"))
    live = jnp.arange(pair_remote.shape[1], dtype=jnp.int32) < pair_count[0]
    result = jnp.zeros((pair_remote.shape[1],) + back[0].shape, jnp.float32)
    for block, remote in zip(back, met):
        chosen = (live & (pair_remote[0] == remote))[:, None, None]
        result = jnp.where(chosen, block[None].astype(jnp.float32), result)
    return result[None, None]


def solution(mesh):
    in_specs = (P(None, ("chan", "win"), None), P("chan", None), P("chan"))
    out_specs = P("win", "chan", None, None, None)
    return jax.shard_map(
        on_device, mesh=mesh, in_specs=in_specs, out_specs=out_specs, check_vma=False
    )
```

```python
import functools
import math

import jax
import jax.numpy as jnp
import ml_dtypes
import numpy as np
from jax import lax
from jax.experimental import pallas as pl
from jax.experimental.pallas import tpu as pltpu
from jax.sharding import PartitionSpec as P

BAND = 64
LAGS = 256
REACH = 2
VMEM = 12 * 2**20
WIDE = 48 * 2**20
MOVES = (2, 1, -1, -2)
ROUTES = len(MOVES)


def lag_table(bins):
    t = np.arange(LAGS) - LAGS // 2
    f = np.arange(bins)
    angle = ((f[:, None] * t[None, :]) % (2 * bins)) * (math.pi / bins)
    table = np.concatenate([np.cos(angle), -np.sin(angle)], axis=0)
    return table.astype(np.float32).astype(ml_dtypes.bfloat16)


def band_matrix():
    row = lax.broadcasted_iota(jnp.int32, (128, 128), 0) // BAND
    column = lax.broadcasted_iota(jnp.int32, (128, 128), 1) // BAND
    return jnp.where(row == column, 1.0, 0.0).astype(jnp.bfloat16)


def whiten_rows(values):
    ones = band_matrix()
    rows, width = values.shape
    bins = width // 2
    real, imag = values[:, :bins], values[:, bins:]
    magnitude = jnp.sqrt(real * real + imag * imag)
    parts = bins // 128
    stacked = jnp.concatenate([magnitude[:, i * 128 : (i + 1) * 128] for i in range(parts)], axis=0)
    high = stacked.astype(jnp.bfloat16)
    low = (stacked - high.astype(jnp.float32)).astype(jnp.bfloat16)
    total = jnp.dot(high, ones, preferred_element_type=jnp.float32) + jnp.dot(
        low, ones, preferred_element_type=jnp.float32
    )
    inverse = 1.0 / (total * (1.0 / BAND) + 1e-06)
    inverse = jnp.concatenate([inverse[i * rows : (i + 1) * rows] for i in range(parts)], axis=1)
    return jnp.concatenate([real * inverse, imag * inverse], axis=1).astype(jnp.bfloat16)


def source_kernel(spectra, out):
    rows = [spectra[w].astype(jnp.float32)[0:1] for w in range(spectra.shape[0])]
    out[...] = whiten_rows(jnp.concatenate(rows, axis=0))


def whiten_kernel(flag, own, sibling, own_out, sibling_out, flag_out, held, done):
    windows = own.shape[0]
    pairs = ((own, own_out), (sibling, sibling_out))
    copies = [
        pltpu.make_async_copy(pairs[k][0].at[w], held.at[k, w], done.at[k, w])
        for w in range(windows)
        for k in range(2)
    ]
    for copy in copies:
        copy.start()
    for i, copy in enumerate(copies):
        w, k = i // 2, i % 2
        copy.wait()
        pairs[k][1][w] = whiten_rows(held[k, w].astype(jnp.float32))
    flag_out[0] = flag[0]


def whiten_source(spectra):
    windows, _, width = spectra.shape
    return pl.pallas_call(
        source_kernel,
        out_shape=jax.ShapeDtypeStruct((windows, width), jnp.bfloat16),
        compiler_params=pltpu.CompilerParams(vmem_limit_bytes=VMEM),
        cost_estimate=pl.CostEstimate(flops=10**6, bytes_accessed=2 * 2**20, transcendentals=0),
        name="whiten_source",
    )(spectra)


def whiten_both(own, sibling, flag):
    windows = own.shape[0]
    shape = jax.ShapeDtypeStruct(own.shape, jnp.bfloat16)
    scalar, whole = pl.BlockSpec(memory_space=pltpu.SMEM), pl.BlockSpec(memory_space=pltpu.VMEM)
    return pl.pallas_call(
        whiten_kernel,
        in_specs=[scalar] + [pl.BlockSpec(memory_space=pltpu.HBM)] * 2,
        out_specs=[whole, whole, scalar],
        out_shape=[shape, shape, jax.ShapeDtypeStruct(flag.shape, flag.dtype)],
        scratch_shapes=[
            pltpu.VMEM((2,) + own.shape, own.dtype),
            pltpu.SemaphoreType.DMA((2, windows)),
        ],
        compiler_params=pltpu.CompilerParams(vmem_limit_bytes=VMEM),
        cost_estimate=pl.CostEstimate(flops=10**9, bytes_accessed=8 * 2**20, transcendentals=0),
        name="whiten_both",
    )(flag, own, sibling)


def correlate_kernel(groups, scale, parity, *refs):
    own, sib = refs[:2]
    sources = refs[2 : 2 + groups]
    table_hbm, out, prod_r, prod_i, src_r, src_i, src_s, table, done = refs[2 + groups :]
    fetch = pltpu.make_async_copy(table_hbm, table, done)
    fetch.start()
    windows, half, width = own.shape
    bins = width // 2
    per = sources[0].shape[0]
    for g, ref in enumerate(sources):
        rows = slice(g * per, (g + 1) * per)
        a, b = ref[:, :, :bins].astype(jnp.float32), ref[:, :, bins:].astype(jnp.float32)
        src_r[rows] = a
        src_i[rows] = b
        src_s[rows] = a + b

    def body(q, carry):
        lanes = pl.ds(pl.multiple_of(q * 128, 128), 128)
        upper = pl.ds(pl.multiple_of(bins + q * 128, 128), 128)
        for h, ref in enumerate((own, sib)):
            place = (parity[0] + h) % 2
            for t in range(0, half, 8):
                chan = []
                for w in range(windows):
                    x = ref[w, :, lanes].astype(jnp.float32)[t : t + 8]
                    y = ref[w, :, upper].astype(jnp.float32)[t : t + 8]
                    chan.append((x, x + y, x - y))
                for s in range(groups * per):
                    total = None
                    for w in range(windows):
                        terms = [
                            jnp.broadcast_to(r[s, w : w + 1, lanes], (8, 128)) * c
                            for r, c in zip((src_s, src_r, src_i), chan[w])
                        ]
                        total = terms if total is None else [p + q for p, q in zip(total, terms)]
                    tile = (s * 2 + place) * (half // 8) + t // 8
                    prod_r[tile, :, lanes] = (total[0] - total[2]).astype(jnp.bfloat16)
                    prod_i[tile, :, lanes] = (total[0] - total[1]).astype(jnp.bfloat16)
        return carry

    def rows(ref):
        return ref[...].reshape(ref.shape[0] * 8, bins)

    lax.fori_loop(0, bins // 128, body, 0)
    fetch.wait()
    total = jnp.dot(rows(prod_r), table[:bins], preferred_element_type=jnp.float32) + jnp.dot(
        rows(prod_i), table[bins:], preferred_element_type=jnp.float32
    )
    out[...] = (total * scale).reshape(out.shape).astype(out.dtype)


def correlate(parity, own, sibling, sources, table, scale):
    windows, half, width = own.shape
    bins = width // 2
    groups, per = len(sources), sources[0].shape[0]
    n = groups * per
    whole = pl.BlockSpec(memory_space=pltpu.VMEM)
    return pl.pallas_call(
        functools.partial(correlate_kernel, groups, scale),
        in_specs=[pl.BlockSpec(memory_space=pltpu.SMEM)] + [whole] * (2 + groups)
        + [pl.BlockSpec(memory_space=pltpu.HBM)],
        out_specs=whole,
        out_shape=jax.ShapeDtypeStruct((n, 2 * half, LAGS), jnp.bfloat16),
        scratch_shapes=[
            pltpu.VMEM((n * 2 * half // 8, 8, bins), jnp.bfloat16),
            pltpu.VMEM((n * 2 * half // 8, 8, bins), jnp.bfloat16),
            pltpu.VMEM((n, windows, bins), jnp.float32),
            pltpu.VMEM((n, windows, bins), jnp.float32),
            pltpu.VMEM((n, windows, bins), jnp.float32),
            pltpu.VMEM(table.shape, table.dtype),
            pltpu.SemaphoreType.DMA,
        ],
        compiler_params=pltpu.CompilerParams(vmem_limit_bytes=WIDE),
        cost_estimate=pl.CostEstimate(
            flops=n * 10**9, bytes_accessed=8 * 2**20, transcendentals=0
        ),
        name=f"correlate_{n}",
    )(parity, own, sibling, *sources, table)


def route_swap(block, move, back=False):
    blocks, size = lax.axis_size("chan"), lax.axis_size("win")
    pairs = []
    for w in range(size):
        for b in range(blocks):
            to = b - move if w % 2 else b + move
            inside = 0 <= to < blocks
            pairs.append((w * blocks + b, w * blocks + to if inside else (w ^ 1) * blocks + b))
    return lax.ppermute(block, ("win", "chan"), [(j, i) if back else (i, j) for i, j in pairs])


def chip_shift(block, distance):
    size = lax.axis_size("win")
    return lax.ppermute(block, "win", [(i, (i + 2 * distance) % size) for i in range(size)])


def core_swap(block):
    size = lax.axis_size("win")
    return lax.ppermute(block, "win", [(i, i ^ 1) for i in range(size)])


def on_device(spectra, pair_remote, pair_count):
    windows, channels, width = spectra.shape
    bins = width // 2
    scale = 1.0 / math.sqrt(bins * windows)
    table = jnp.asarray(lag_table(bins))
    parity = (lax.axis_index("win") % 2).astype(jnp.int32)[None]

    other = core_swap(spectra)
    source = whiten_source(spectra)
    arrived = [route_swap(source, move) for move in MOVES]
    own, sibling, pair_count = whiten_both(spectra, other, pair_count)
    arrived, pair_count = lax.optimization_barrier((arrived, pair_count))
    half = ROUTES // 2
    first, second = jnp.stack(arrived[:half]), jnp.stack(arrived[half:])

    up_first, down_first = chip_shift(first, 1), chip_shift(first, -1)
    up_second, down_second = chip_shift(second, 1), chip_shift(second, -1)
    run = functools.partial(correlate, parity, own, sibling, table=table, scale=scale)
    own_first = run([first])
    own_first, up_first, down_first = lax.optimization_barrier((own_first, up_first, down_first))
    far_first = chip_shift(up_first, 1)
    near_first = run([up_first, down_first])
    near_first, up_second, down_second = lax.optimization_barrier(
        (near_first, up_second, down_second)
    )
    far_second = chip_shift(down_second, -1)
    near_second = run([up_second, down_second])
    near_second, far_first, far_second = lax.optimization_barrier(
        (near_second, far_first, far_second)
    )
    c_far = run([far_first, far_second])
    c_far, second = lax.optimization_barrier((c_far, second))
    c_own = jnp.concatenate([own_first, run([second])])
    c_up = jnp.concatenate([near_first[:half], near_second[:half]])
    c_down = jnp.concatenate([near_first[half:], near_second[half:]])

    chips = lax.axis_size("win") // 2
    chip = lax.axis_index("win") // 2
    home = [c_own, chip_shift(c_down, 1), chip_shift(c_far, 2), chip_shift(c_up, -1)]
    stacked = jnp.stack(home)
    order = (chip - jnp.arange(chips)) % chips
    stacked = stacked[order]
    blocks = jnp.swapaxes(stacked, 0, 1).reshape(ROUTES, chips * 2 * channels, LAGS)
    back = [route_swap(blocks[i], move, back=True) for i, move in enumerate(MOVES)]

    here, sign = lax.axis_index("chan"), 1 - 2 * parity[0]
    live = jnp.arange(pair_remote.shape[1], dtype=jnp.int32) < pair_count[0]
    result = jnp.zeros((pair_remote.shape[1],) + back[0].shape, jnp.float32)
    for block, move in zip(back, MOVES):
        chosen = (live & (pair_remote[0] == here + move * sign))[:, None, None]
        result = jnp.where(chosen, block[None].astype(jnp.float32), result)
    return result[None, None]


def solution(mesh):
    in_specs = (P(None, ("chan", "win"), None), P("chan", None), P("chan"))
    out_specs = P("win", "chan", None, None, None)
    return jax.shard_map(
        on_device, mesh=mesh, in_specs=in_specs, out_specs=out_specs, check_vma=False
    )
```

```python
import functools
import math

import jax
import jax.numpy as jnp
import ml_dtypes
import numpy as np
from jax import lax
from jax.experimental import pallas as pl
from jax.experimental.pallas import tpu as pltpu
from jax.sharding import PartitionSpec as P

BAND = 64
LAGS = 256
REACH = 2
VMEM = 12 * 2**20
WIDE = 48 * 2**20
MOVES = (1, 2, -1, -2)
ROUTES = len(MOVES)


def lag_table(bins):
    t = np.arange(LAGS) - LAGS // 2
    f = np.arange(bins)
    angle = ((f[:, None] * t[None, :]) % (2 * bins)) * (math.pi / bins)
    table = np.concatenate([np.cos(angle), -np.sin(angle)], axis=0)
    return table.astype(np.float32).astype(ml_dtypes.bfloat16)


def band_matrix():
    row = lax.broadcasted_iota(jnp.int32, (128, 128), 0) // BAND
    column = lax.broadcasted_iota(jnp.int32, (128, 128), 1) // BAND
    return jnp.where(row == column, 1.0, 0.0).astype(jnp.bfloat16)


def whiten_rows(values):
    ones = band_matrix()
    rows, width = values.shape
    bins = width // 2
    parts = bins // 128
    split = [
        (values[:, i * 128 : (i + 1) * 128], values[:, bins + i * 128 : bins + (i + 1) * 128])
        for i in range(parts)
    ]
    powers = [re * re + im * im for re, im in split]
    stacked = jnp.concatenate([p * lax.rsqrt(jnp.maximum(p, 1e-30)) for p in powers], axis=0)
    high = stacked.astype(jnp.bfloat16)
    low = (stacked - high.astype(jnp.float32)).astype(jnp.bfloat16)
    total = jnp.dot(
        jnp.concatenate([high, low], axis=1),
        jnp.concatenate([ones, ones], axis=0),
        preferred_element_type=jnp.float32,
    )
    inverse = 1.0 / (total * (1.0 / BAND) + 1e-06)
    scaled = [inverse[i * rows : (i + 1) * rows] for i in range(parts)]
    real = [re * k for (re, _), k in zip(split, scaled)]
    imag = [im * k for (_, im), k in zip(split, scaled)]
    return jnp.concatenate(real + imag, axis=1).astype(jnp.bfloat16)


def source_kernel(spectra, out, held, done):
    windows = spectra.shape[0]
    copies = [pltpu.make_async_copy(spectra.at[w], held.at[w], done.at[w]) for w in range(windows)]
    for copy in copies:
        copy.start()
    rows = []
    for w, copy in enumerate(copies):
        copy.wait()
        rows.append(held[w].astype(jnp.float32)[0:1])
    out[...] = whiten_rows(jnp.concatenate(rows, axis=0))


def whiten_kernel(flag, own, sibling, own_out, sibling_out, flag_out, held, done):
    windows = own.shape[0]
    pairs = ((own, own_out), (sibling, sibling_out))

    def fetch(k, w):
        return pltpu.make_async_copy(pairs[k][0].at[w], held.at[k, w], done.at[k, w])

    for w in range(windows):
        for k in range(2):
            fetch(k, w).start()

    def body(w, carry):
        for k in range(2):
            fetch(k, w).wait()
            pairs[k][1][w] = whiten_rows(held[k, w].astype(jnp.float32))
        return carry

    lax.fori_loop(0, windows, body, 0)
    flag_out[0] = flag[0]


def whiten_source(spectra):
    windows, _, width = spectra.shape
    return pl.pallas_call(
        source_kernel,
        in_specs=[pl.BlockSpec(memory_space=pltpu.HBM)],
        out_specs=pl.BlockSpec(memory_space=pltpu.VMEM),
        scratch_shapes=[
            pltpu.VMEM(spectra.shape, spectra.dtype),
            pltpu.SemaphoreType.DMA((windows,)),
        ],
        out_shape=jax.ShapeDtypeStruct((windows, width), jnp.bfloat16),
        compiler_params=pltpu.CompilerParams(vmem_limit_bytes=VMEM),
        cost_estimate=pl.CostEstimate(flops=10**6, bytes_accessed=2 * 2**20, transcendentals=0),
        name="whiten_source",
    )(spectra)


def whiten_both(own, sibling, flag):
    windows = own.shape[0]
    shape = jax.ShapeDtypeStruct(own.shape, jnp.bfloat16)
    scalar, whole = pl.BlockSpec(memory_space=pltpu.SMEM), pl.BlockSpec(memory_space=pltpu.VMEM)
    return pl.pallas_call(
        whiten_kernel,
        in_specs=[scalar] + [pl.BlockSpec(memory_space=pltpu.HBM)] * 2,
        out_specs=[whole, whole, scalar],
        out_shape=[shape, shape, jax.ShapeDtypeStruct(flag.shape, flag.dtype)],
        scratch_shapes=[
            pltpu.VMEM((2,) + own.shape, own.dtype),
            pltpu.SemaphoreType.DMA((2, windows)),
        ],
        compiler_params=pltpu.CompilerParams(vmem_limit_bytes=VMEM),
        cost_estimate=pl.CostEstimate(flops=10**9, bytes_accessed=8 * 2**20, transcendentals=0),
        name="whiten_both",
    )(flag, own, sibling)


def correlate_kernel(groups, scale, parity, *refs):
    own, sib = refs[:2]
    sources = refs[2 : 2 + groups]
    table_hbm, out, prod_r, prod_i, src_r, src_i, src_s, table, done = refs[2 + groups :]
    fetch = pltpu.make_async_copy(table_hbm, table, done)
    fetch.start()
    windows, half, width = own.shape
    bins = width // 2
    per = sources[0].shape[0]
    for g, ref in enumerate(sources):
        rows = slice(g * per, (g + 1) * per)
        a, b = ref[:, :, :bins].astype(jnp.float32), ref[:, :, bins:].astype(jnp.float32)
        src_r[rows] = a
        src_i[rows] = b
        src_s[rows] = a + b

    def body(q, carry):
        lanes = pl.ds(pl.multiple_of(q * 128, 128), 128)
        upper = pl.ds(pl.multiple_of(bins + q * 128, 128), 128)
        for h, ref in enumerate((own, sib)):
            place = (parity[0] + h) % 2
            for t in range(0, half, 8):
                chan = []
                for w in range(windows):
                    x = ref[w, :, lanes].astype(jnp.float32)[t : t + 8]
                    y = ref[w, :, upper].astype(jnp.float32)[t : t + 8]
                    chan.append((x, x + y, x - y))
                for s in range(groups * per):
                    total = None
                    for w in range(windows):
                        terms = [
                            jnp.broadcast_to(r[s, w : w + 1, lanes], (8, 128)) * c
                            for r, c in zip((src_s, src_r, src_i), chan[w])
                        ]
                        total = terms if total is None else [p + q for p, q in zip(total, terms)]
                    tile = (s * 2 + place) * (half // 8) + t // 8
                    prod_r[tile, :, lanes] = (total[0] - total[2]).astype(jnp.bfloat16)
                    prod_i[tile, :, lanes] = (total[0] - total[1]).astype(jnp.bfloat16)
        return carry

    def rows(ref):
        return ref[...].reshape(ref.shape[0] * 8, bins)

    lax.fori_loop(0, bins // 128, body, 0)
    fetch.wait()
    total = jnp.dot(rows(prod_r), table[:bins], preferred_element_type=jnp.float32) + jnp.dot(
        rows(prod_i), table[bins:], preferred_element_type=jnp.float32
    )
    out[...] = (total * scale).reshape(out.shape).astype(out.dtype)


def correlate(parity, own, sibling, sources, table, scale):
    windows, half, width = own.shape
    bins = width // 2
    groups, per = len(sources), sources[0].shape[0]
    n = groups * per
    whole = pl.BlockSpec(memory_space=pltpu.VMEM)
    return pl.pallas_call(
        functools.partial(correlate_kernel, groups, scale),
        in_specs=[pl.BlockSpec(memory_space=pltpu.SMEM)] + [whole] * (2 + groups)
        + [pl.BlockSpec(memory_space=pltpu.HBM)],
        out_specs=whole,
        out_shape=jax.ShapeDtypeStruct((n, 2 * half, LAGS), jnp.bfloat16),
        scratch_shapes=[
            pltpu.VMEM((n * 2 * half // 8, 8, bins), jnp.bfloat16),
            pltpu.VMEM((n * 2 * half // 8, 8, bins), jnp.bfloat16),
            pltpu.VMEM((n, windows, bins), jnp.float32),
            pltpu.VMEM((n, windows, bins), jnp.float32),
            pltpu.VMEM((n, windows, bins), jnp.float32),
            pltpu.VMEM(table.shape, table.dtype),
            pltpu.SemaphoreType.DMA,
        ],
        compiler_params=pltpu.CompilerParams(vmem_limit_bytes=WIDE),
        cost_estimate=pl.CostEstimate(
            flops=n * 10**9, bytes_accessed=8 * 2**20, transcendentals=0
        ),
        name=f"correlate_{n}",
    )(parity, own, sibling, *sources, table)


def route_swap(block, move, back=False):
    blocks, size = lax.axis_size("chan"), lax.axis_size("win")
    pairs = []
    for w in range(size):
        for b in range(blocks):
            to = b - move if w % 2 else b + move
            inside = 0 <= to < blocks
            pairs.append((w * blocks + b, w * blocks + to if inside else (w ^ 1) * blocks + b))
    return lax.ppermute(block, ("win", "chan"), [(j, i) if back else (i, j) for i, j in pairs])


def chip_shift(block, distance):
    size = lax.axis_size("win")
    return lax.ppermute(block, "win", [(i, (i + 2 * distance) % size) for i in range(size)])


def core_swap(block):
    size = lax.axis_size("win")
    return lax.ppermute(block, "win", [(i, i ^ 1) for i in range(size)])


def on_device(spectra, pair_remote, pair_count):
    windows, channels, width = spectra.shape
    bins = width // 2
    scale = 1.0 / math.sqrt(bins * windows)
    table = jnp.asarray(lag_table(bins))
    parity = (lax.axis_index("win") % 2).astype(jnp.int32)[None]

    other = core_swap(spectra)
    source = whiten_source(spectra)
    arrived = [route_swap(source, move) for move in MOVES]
    own, sibling, pair_count = whiten_both(spectra, other, pair_count)
    arrived, pair_count = lax.optimization_barrier((arrived, pair_count))
    half = ROUTES // 2
    first, second = jnp.stack(arrived[:half]), jnp.stack(arrived[half:])

    up_first, down_first = chip_shift(first, 1), chip_shift(first, -1)
    up_second, down_second = chip_shift(second, 1), chip_shift(second, -1)
    run = functools.partial(correlate, parity, own, sibling, table=table, scale=scale)
    own_first = run([first])
    own_first, up_first, down_first = lax.optimization_barrier((own_first, up_first, down_first))
    far_first = chip_shift(up_first, 1)
    near_first = run([up_first, down_first])
    near_first, up_second, down_second = lax.optimization_barrier(
        (near_first, up_second, down_second)
    )
    far_second = chip_shift(down_second, -1)
    near_second = run([up_second, down_second])
    near_second, far_first, far_second = lax.optimization_barrier(
        (near_second, far_first, far_second)
    )
    c_far = run([far_first, far_second])
    c_far, second = lax.optimization_barrier((c_far, second))
    c_own = jnp.concatenate([own_first, run([second])])
    c_up = jnp.concatenate([near_first[:half], near_second[:half]])
    c_down = jnp.concatenate([near_first[half:], near_second[half:]])

    chips = lax.axis_size("win") // 2
    chip = lax.axis_index("win") // 2
    home = [c_own, chip_shift(c_down, 1), chip_shift(c_far, 2), chip_shift(c_up, -1)]
    stacked = jnp.stack(home)
    order = (chip - jnp.arange(chips)) % chips
    stacked = stacked[order]
    blocks = jnp.swapaxes(stacked, 0, 1).reshape(ROUTES, chips * 2 * channels, LAGS)
    back = [route_swap(blocks[i], move, back=True) for i, move in enumerate(MOVES)]

    here, sign = lax.axis_index("chan"), 1 - 2 * parity[0]
    live = jnp.arange(pair_remote.shape[1], dtype=jnp.int32) < pair_count[0]
    result = jnp.zeros((pair_remote.shape[1],) + back[0].shape, jnp.float32)
    for block, move in zip(back, MOVES):
        chosen = (live & (pair_remote[0] == here + move * sign))[:, None, None]
        result = jnp.where(chosen, block[None].astype(jnp.float32), result)
    return result[None, None]


def solution(mesh):
    in_specs = (P(None, ("chan", "win"), None), P("chan", None), P("chan"))
    out_specs = P("win", "chan", None, None, None)
    return jax.shard_map(
        on_device, mesh=mesh, in_specs=in_specs, out_specs=out_specs, check_vma=False
    )
```

```python
import functools
import math

import jax
import jax.numpy as jnp
import ml_dtypes
import numpy as np
from jax import lax
from jax.experimental import pallas as pl
from jax.experimental.pallas import tpu as pltpu
from jax.sharding import PartitionSpec as P

BAND = 64
LAGS = 256
REACH = 2
VMEM = 12 * 2**20
WIDE = 48 * 2**20
MOVES = (1, 2, -1, -2)
ROUTES = len(MOVES)


def lag_table(bins):
    t = np.arange(LAGS) - LAGS // 2
    f = np.arange(bins)
    angle = ((f[:, None] * t[None, :]) % (2 * bins)) * (math.pi / bins)
    table = np.concatenate([np.cos(angle), -np.sin(angle)], axis=0)
    return table.astype(np.float32).astype(ml_dtypes.bfloat16)


def band_matrix():
    row = lax.broadcasted_iota(jnp.int32, (128, 128), 0) // BAND
    column = lax.broadcasted_iota(jnp.int32, (128, 128), 1) // BAND
    return jnp.where(row == column, 1.0, 0.0).astype(jnp.bfloat16)


def whiten_rows(values):
    ones = band_matrix()
    rows, width = values.shape
    bins = width // 2
    parts = bins // 128
    split = [
        (values[:, i * 128 : (i + 1) * 128], values[:, bins + i * 128 : bins + (i + 1) * 128])
        for i in range(parts)
    ]
    powers = [re * re + im * im for re, im in split]
    stacked = jnp.concatenate([p * lax.rsqrt(jnp.maximum(p, 1e-30)) for p in powers], axis=0)
    high = stacked.astype(jnp.bfloat16)
    low = (stacked - high.astype(jnp.float32)).astype(jnp.bfloat16)
    total = jnp.dot(
        jnp.concatenate([high, low], axis=1),
        jnp.concatenate([ones, ones], axis=0),
        preferred_element_type=jnp.float32,
    )
    inverse = 1.0 / (total * (1.0 / BAND) + 1e-06)
    scaled = [inverse[i * rows : (i + 1) * rows] for i in range(parts)]
    real = [re * k for (re, _), k in zip(split, scaled)]
    imag = [im * k for (_, im), k in zip(split, scaled)]
    return jnp.concatenate(real + imag, axis=1).astype(jnp.bfloat16)


def source_kernel(spectra, out, held, done):
    windows = spectra.shape[0]
    copies = [pltpu.make_async_copy(spectra.at[w], held.at[w], done.at[w]) for w in range(windows)]
    for copy in copies:
        copy.start()
    rows = []
    for w, copy in enumerate(copies):
        copy.wait()
        rows.append(held[w].astype(jnp.float32)[0:1])
    out[...] = whiten_rows(jnp.concatenate(rows, axis=0))


def whiten_kernel(flag, own, sibling, own_out, sibling_out, flag_out, held, done):
    windows = own.shape[0]
    pairs = ((own, own_out), (sibling, sibling_out))

    def fetch(k, w):
        return pltpu.make_async_copy(pairs[k][0].at[w], held.at[k, w], done.at[k, w])

    for w in range(windows):
        for k in range(2):
            fetch(k, w).start()

    def body(w, carry):
        for k in range(2):
            fetch(k, w).wait()
            pairs[k][1][w] = whiten_rows(held[k, w].astype(jnp.float32))
        return carry

    lax.fori_loop(0, windows, body, 0)
    flag_out[0] = flag[0]


def whiten_source(spectra):
    windows, _, width = spectra.shape
    return pl.pallas_call(
        source_kernel,
        in_specs=[pl.BlockSpec(memory_space=pltpu.HBM)],
        out_specs=pl.BlockSpec(memory_space=pltpu.VMEM),
        scratch_shapes=[
            pltpu.VMEM(spectra.shape, spectra.dtype),
            pltpu.SemaphoreType.DMA((windows,)),
        ],
        out_shape=jax.ShapeDtypeStruct((windows, width), jnp.bfloat16),
        compiler_params=pltpu.CompilerParams(vmem_limit_bytes=VMEM),
        cost_estimate=pl.CostEstimate(flops=10**6, bytes_accessed=2 * 2**20, transcendentals=0),
        name="whiten_source",
    )(spectra)


def whiten_both(own, sibling, flag):
    windows = own.shape[0]
    shape = jax.ShapeDtypeStruct(own.shape, jnp.bfloat16)
    scalar, whole = pl.BlockSpec(memory_space=pltpu.SMEM), pl.BlockSpec(memory_space=pltpu.VMEM)
    return pl.pallas_call(
        whiten_kernel,
        in_specs=[scalar] + [pl.BlockSpec(memory_space=pltpu.HBM)] * 2,
        out_specs=[whole, whole, scalar],
        out_shape=[shape, shape, jax.ShapeDtypeStruct(flag.shape, flag.dtype)],
        scratch_shapes=[
            pltpu.VMEM((2,) + own.shape, own.dtype),
            pltpu.SemaphoreType.DMA((2, windows)),
        ],
        compiler_params=pltpu.CompilerParams(vmem_limit_bytes=VMEM),
        cost_estimate=pl.CostEstimate(flops=10**9, bytes_accessed=8 * 2**20, transcendentals=0),
        name="whiten_both",
    )(flag, own, sibling)


def correlate_kernel(groups, scale, parity, *refs):
    own, sib = refs[:2]
    sources = refs[2 : 2 + groups]
    table_hbm, out, prod_r, prod_i, src_r, src_i, src_s, table, done = refs[2 + groups :]
    fetch = pltpu.make_async_copy(table_hbm, table, done)
    fetch.start()
    windows, half, width = own.shape
    bins = width // 2
    per = sources[0].shape[0]
    for g, ref in enumerate(sources):
        rows = slice(g * per, (g + 1) * per)
        a, b = ref[:, :, :bins].astype(jnp.float32), ref[:, :, bins:].astype(jnp.float32)
        src_r[rows] = a
        src_i[rows] = b
        src_s[rows] = a + b

    def body(q, carry):
        lanes = pl.ds(pl.multiple_of(q * 128, 128), 128)
        upper = pl.ds(pl.multiple_of(bins + q * 128, 128), 128)
        for h, ref in enumerate((own, sib)):
            place = (parity[0] + h) % 2
            for t in range(0, half, 8):
                chan = []
                for w in range(windows):
                    x = ref[w, :, lanes].astype(jnp.float32)[t : t + 8]
                    y = ref[w, :, upper].astype(jnp.float32)[t : t + 8]
                    chan.append((x, x + y, x - y))
                for s in range(groups * per):
                    total = None
                    for w in range(windows):
                        terms = [
                            jnp.broadcast_to(r[s, w : w + 1, lanes], (8, 128)) * c
                            for r, c in zip((src_s, src_r, src_i), chan[w])
                        ]
                        total = terms if total is None else [p + q for p, q in zip(total, terms)]
                    tile = (s * 2 + place) * (half // 8) + t // 8
                    prod_r[tile, :, lanes] = (total[0] - total[2]).astype(jnp.bfloat16)
                    prod_i[tile, :, lanes] = (total[0] - total[1]).astype(jnp.bfloat16)
        return carry

    def rows(ref):
        return ref[...].reshape(ref.shape[0] * 8, bins)

    lax.fori_loop(0, bins // 128, body, 0)
    fetch.wait()
    total = jnp.dot(rows(prod_r), table[:bins], preferred_element_type=jnp.float32) + jnp.dot(
        rows(prod_i), table[bins:], preferred_element_type=jnp.float32
    )
    out[...] = (total * scale).reshape(out.shape).astype(out.dtype)


def correlate(parity, own, sibling, sources, table, scale):
    windows, half, width = own.shape
    bins = width // 2
    groups, per = len(sources), sources[0].shape[0]
    n = groups * per
    whole = pl.BlockSpec(memory_space=pltpu.VMEM)
    return pl.pallas_call(
        functools.partial(correlate_kernel, groups, scale),
        in_specs=[pl.BlockSpec(memory_space=pltpu.SMEM)] + [whole] * (2 + groups)
        + [pl.BlockSpec(memory_space=pltpu.HBM)],
        out_specs=whole,
        out_shape=jax.ShapeDtypeStruct((n, 2 * half, LAGS), jnp.bfloat16),
        scratch_shapes=[
            pltpu.VMEM((n * 2 * half // 8, 8, bins), jnp.bfloat16),
            pltpu.VMEM((n * 2 * half // 8, 8, bins), jnp.bfloat16),
            pltpu.VMEM((n, windows, bins), jnp.float32),
            pltpu.VMEM((n, windows, bins), jnp.float32),
            pltpu.VMEM((n, windows, bins), jnp.float32),
            pltpu.VMEM(table.shape, table.dtype),
            pltpu.SemaphoreType.DMA,
        ],
        compiler_params=pltpu.CompilerParams(vmem_limit_bytes=WIDE),
        cost_estimate=pl.CostEstimate(
            flops=n * 10**9, bytes_accessed=8 * 2**20, transcendentals=0
        ),
        name=f"correlate_{n}",
    )(parity, own, sibling, *sources, table)


def route_swap(block, move, back=False):
    blocks, size = lax.axis_size("chan"), lax.axis_size("win")
    pairs = []
    for w in range(size):
        for b in range(blocks):
            to = b - move if w % 2 else b + move
            inside = 0 <= to < blocks
            pairs.append((w * blocks + b, w * blocks + to if inside else (w ^ 1) * blocks + b))
    return lax.ppermute(block, ("win", "chan"), [(j, i) if back else (i, j) for i, j in pairs])


def chip_shift(block, distance):
    size = lax.axis_size("win")
    return lax.ppermute(block, "win", [(i, (i + 2 * distance) % size) for i in range(size)])


def core_swap(block):
    size = lax.axis_size("win")
    return lax.ppermute(block, "win", [(i, i ^ 1) for i in range(size)])


def on_device(spectra, pair_remote, pair_count):
    windows, channels, width = spectra.shape
    bins = width // 2
    scale = 1.0 / math.sqrt(bins * windows)
    table = jnp.asarray(lag_table(bins))
    parity = (lax.axis_index("win") % 2).astype(jnp.int32)[None]

    other = core_swap(spectra)
    source = whiten_source(spectra)
    arrived = [route_swap(source, move) for move in MOVES]
    own, sibling, pair_count = whiten_both(spectra, other, pair_count)
    arrived, pair_count = lax.optimization_barrier((arrived, pair_count))
    half = ROUTES // 2
    first, second = jnp.stack(arrived[:half]), jnp.stack(arrived[half:])

    up_first, down_first = chip_shift(first, 1), chip_shift(first, -1)
    run = functools.partial(correlate, parity, own, sibling, table=table, scale=scale)
    own_first = run([first])
    own_first, second = lax.optimization_barrier((own_first, second))
    up_second, down_second = chip_shift(second, 1), chip_shift(second, -1)
    own_first, up_first, down_first = lax.optimization_barrier((own_first, up_first, down_first))
    far_first = chip_shift(up_first, 1)
    near_first = run([up_first, down_first])
    near_first, up_second, down_second = lax.optimization_barrier(
        (near_first, up_second, down_second)
    )
    far_second = chip_shift(down_second, -1)
    near_second = run([up_second, down_second])
    near_second, far_first, far_second = lax.optimization_barrier(
        (near_second, far_first, far_second)
    )
    c_far = run([far_first, far_second])
    c_far, second = lax.optimization_barrier((c_far, second))
    c_own = jnp.concatenate([own_first, run([second])])
    c_up = jnp.concatenate([near_first[:half], near_second[:half]])
    c_down = jnp.concatenate([near_first[half:], near_second[half:]])

    chips = lax.axis_size("win") // 2
    chip = lax.axis_index("win") // 2
    home = [c_own, chip_shift(c_down, 1), chip_shift(c_far, 2), chip_shift(c_up, -1)]
    stacked = jnp.stack(home)
    order = (chip - jnp.arange(chips)) % chips
    stacked = stacked[order]
    blocks = jnp.swapaxes(stacked, 0, 1).reshape(ROUTES, chips * 2 * channels, LAGS)
    back = [route_swap(blocks[i], move, back=True) for i, move in enumerate(MOVES)]

    here, sign = lax.axis_index("chan"), 1 - 2 * parity[0]
    live = jnp.arange(pair_remote.shape[1], dtype=jnp.int32) < pair_count[0]
    result = jnp.zeros((pair_remote.shape[1],) + back[0].shape, jnp.float32)
    for block, move in zip(back, MOVES):
        chosen = (live & (pair_remote[0] == here + move * sign))[:, None, None]
        result = jnp.where(chosen, block[None].astype(jnp.float32), result)
    return result[None, None]


def solution(mesh):
    in_specs = (P(None, ("chan", "win"), None), P("chan", None), P("chan"))
    out_specs = P("win", "chan", None, None, None)
    return jax.shard_map(
        on_device, mesh=mesh, in_specs=in_specs, out_specs=out_specs, check_vma=False
    )
```

```python
import functools
import math

import jax
import jax.numpy as jnp
import ml_dtypes
import numpy as np
from jax import lax
from jax.experimental import pallas as pl
from jax.experimental.pallas import tpu as pltpu
from jax.sharding import PartitionSpec as P

BAND = 64
LAGS = 256
REACH = 2
VMEM = 12 * 2**20
WIDE = 48 * 2**20
MOVES = (1, 2, -1, -2)
ROUTES = len(MOVES)


def lag_table(bins):
    t = np.arange(LAGS) - LAGS // 2
    f = np.arange(bins)
    angle = ((f[:, None] * t[None, :]) % (2 * bins)) * (math.pi / bins)
    table = np.concatenate([np.cos(angle), -np.sin(angle)], axis=0)
    return table.astype(np.float32).astype(ml_dtypes.bfloat16)


def band_matrix():
    row = lax.broadcasted_iota(jnp.int32, (128, 128), 0) // BAND
    column = lax.broadcasted_iota(jnp.int32, (128, 128), 1) // BAND
    return jnp.where(row == column, 1.0, 0.0).astype(jnp.bfloat16)


def whiten_rows(values):
    ones = band_matrix()
    rows, width = values.shape
    bins = width // 2
    parts = bins // 128
    split = [
        (values[:, i * 128 : (i + 1) * 128], values[:, bins + i * 128 : bins + (i + 1) * 128])
        for i in range(parts)
    ]
    powers = [re * re + im * im for re, im in split]
    stacked = jnp.concatenate([p * lax.rsqrt(jnp.maximum(p, 1e-30)) for p in powers], axis=0)
    high = stacked.astype(jnp.bfloat16)
    low = (stacked - high.astype(jnp.float32)).astype(jnp.bfloat16)
    total = jnp.dot(
        jnp.concatenate([high, low], axis=1),
        jnp.concatenate([ones, ones], axis=0),
        preferred_element_type=jnp.float32,
    )
    inverse = 1.0 / (total * (1.0 / BAND) + 1e-06)
    scaled = [inverse[i * rows : (i + 1) * rows] for i in range(parts)]
    real = [re * k for (re, _), k in zip(split, scaled)]
    imag = [im * k for (_, im), k in zip(split, scaled)]
    return jnp.concatenate(real + imag, axis=1).astype(jnp.bfloat16)


def source_kernel(spectra, out, held, done):
    windows = spectra.shape[0]
    copies = [pltpu.make_async_copy(spectra.at[w], held.at[w], done.at[w]) for w in range(windows)]
    for copy in copies:
        copy.start()
    rows = []
    for w, copy in enumerate(copies):
        copy.wait()
        rows.append(held[w].astype(jnp.float32)[0:1])
    out[...] = whiten_rows(jnp.concatenate(rows, axis=0))


def whiten_kernel(flag, own, sibling, own_out, sibling_out, flag_out, held, done):
    windows = own.shape[0]
    pairs = ((own, own_out), (sibling, sibling_out))

    def fetch(k, w):
        return pltpu.make_async_copy(pairs[k][0].at[w], held.at[k, w], done.at[k, w])

    for w in range(windows):
        for k in range(2):
            fetch(k, w).start()

    def body(w, carry):
        for k in range(2):
            fetch(k, w).wait()
            pairs[k][1][w] = whiten_rows(held[k, w].astype(jnp.float32))
        return carry

    lax.fori_loop(0, windows, body, 0)
    flag_out[0] = flag[0]


def whiten_source(spectra):
    windows, _, width = spectra.shape
    return pl.pallas_call(
        source_kernel,
        in_specs=[pl.BlockSpec(memory_space=pltpu.HBM)],
        out_specs=pl.BlockSpec(memory_space=pltpu.VMEM),
        scratch_shapes=[
            pltpu.VMEM(spectra.shape, spectra.dtype),
            pltpu.SemaphoreType.DMA((windows,)),
        ],
        out_shape=jax.ShapeDtypeStruct((windows, width), jnp.bfloat16),
        compiler_params=pltpu.CompilerParams(vmem_limit_bytes=VMEM),
        cost_estimate=pl.CostEstimate(flops=10**6, bytes_accessed=2 * 2**20, transcendentals=0),
        name="whiten_source",
    )(spectra)


def whiten_both(own, sibling, flag):
    windows = own.shape[0]
    shape = jax.ShapeDtypeStruct(own.shape, jnp.bfloat16)
    scalar, whole = pl.BlockSpec(memory_space=pltpu.SMEM), pl.BlockSpec(memory_space=pltpu.VMEM)
    return pl.pallas_call(
        whiten_kernel,
        in_specs=[scalar] + [pl.BlockSpec(memory_space=pltpu.HBM)] * 2,
        out_specs=[whole, whole, scalar],
        out_shape=[shape, shape, jax.ShapeDtypeStruct(flag.shape, flag.dtype)],
        scratch_shapes=[
            pltpu.VMEM((2,) + own.shape, own.dtype),
            pltpu.SemaphoreType.DMA((2, windows)),
        ],
        compiler_params=pltpu.CompilerParams(vmem_limit_bytes=VMEM),
        cost_estimate=pl.CostEstimate(flops=10**9, bytes_accessed=8 * 2**20, transcendentals=0),
        name="whiten_both",
    )(flag, own, sibling)


def correlate_kernel(groups, scale, parity, *refs):
    own, sib = refs[:2]
    sources = refs[2 : 2 + groups]
    table_hbm, out, prod_r, prod_i, src_r, src_i, src_s, table, done = refs[2 + groups :]
    fetch = pltpu.make_async_copy(table_hbm, table, done)
    fetch.start()
    windows, half, width = own.shape
    bins = width // 2
    per = sources[0].shape[0]
    for g, ref in enumerate(sources):
        rows = slice(g * per, (g + 1) * per)
        a, b = ref[:, :, :bins].astype(jnp.float32), ref[:, :, bins:].astype(jnp.float32)
        src_r[rows] = a
        src_i[rows] = b
        src_s[rows] = a + b

    def body(q, carry):
        lanes = pl.ds(pl.multiple_of(q * 128, 128), 128)
        upper = pl.ds(pl.multiple_of(bins + q * 128, 128), 128)
        for h, ref in enumerate((own, sib)):
            place = (parity[0] + h) % 2
            for t in range(0, half, 8):
                chan = []
                for w in range(windows):
                    x = ref[w, :, lanes].astype(jnp.float32)[t : t + 8]
                    y = ref[w, :, upper].astype(jnp.float32)[t : t + 8]
                    chan.append((x, x + y, x - y))
                for s in range(groups * per):
                    total = None
                    for w in range(windows):
                        terms = [
                            jnp.broadcast_to(r[s, w : w + 1, lanes], (8, 128)) * c
                            for r, c in zip((src_s, src_r, src_i), chan[w])
                        ]
                        total = terms if total is None else [p + q for p, q in zip(total, terms)]
                    tile = (s * 2 + place) * (half // 8) + t // 8
                    prod_r[tile, :, lanes] = (total[0] - total[2]).astype(jnp.bfloat16)
                    prod_i[tile, :, lanes] = (total[0] - total[1]).astype(jnp.bfloat16)
        return carry

    def rows(ref):
        return ref[...].reshape(ref.shape[0] * 8, bins)

    lax.fori_loop(0, bins // 128, body, 0)
    fetch.wait()
    total = jnp.dot(rows(prod_r), table[:bins], preferred_element_type=jnp.float32) + jnp.dot(
        rows(prod_i), table[bins:], preferred_element_type=jnp.float32
    )
    out[...] = (total * scale).reshape(out.shape).astype(out.dtype)


def correlate(parity, own, sibling, sources, table, scale):
    windows, half, width = own.shape
    bins = width // 2
    groups, per = len(sources), sources[0].shape[0]
    n = groups * per
    whole = pl.BlockSpec(memory_space=pltpu.VMEM)
    return pl.pallas_call(
        functools.partial(correlate_kernel, groups, scale),
        in_specs=[pl.BlockSpec(memory_space=pltpu.SMEM)] + [whole] * (2 + groups)
        + [pl.BlockSpec(memory_space=pltpu.HBM)],
        out_specs=whole,
        out_shape=jax.ShapeDtypeStruct((n, 2 * half, LAGS), jnp.bfloat16),
        scratch_shapes=[
            pltpu.VMEM((n * 2 * half // 8, 8, bins), jnp.bfloat16),
            pltpu.VMEM((n * 2 * half // 8, 8, bins), jnp.bfloat16),
            pltpu.VMEM((n, windows, bins), jnp.float32),
            pltpu.VMEM((n, windows, bins), jnp.float32),
            pltpu.VMEM((n, windows, bins), jnp.float32),
            pltpu.VMEM(table.shape, table.dtype),
            pltpu.SemaphoreType.DMA,
        ],
        compiler_params=pltpu.CompilerParams(vmem_limit_bytes=WIDE),
        cost_estimate=pl.CostEstimate(
            flops=n * 10**9, bytes_accessed=8 * 2**20, transcendentals=0
        ),
        name=f"correlate_{n}",
    )(parity, own, sibling, *sources, table)


def route_swap(block, move, back=False):
    blocks, size = lax.axis_size("chan"), lax.axis_size("win")
    pairs = []
    for w in range(size):
        for b in range(blocks):
            to = b - move if w % 2 else b + move
            inside = 0 <= to < blocks
            pairs.append((w * blocks + b, w * blocks + to if inside else (w ^ 1) * blocks + b))
    return lax.ppermute(block, ("win", "chan"), [(j, i) if back else (i, j) for i, j in pairs])


def chip_shift(block, distance):
    size = lax.axis_size("win")
    return lax.ppermute(block, "win", [(i, (i + 2 * distance) % size) for i in range(size)])


def core_swap(block):
    size = lax.axis_size("win")
    return lax.ppermute(block, "win", [(i, i ^ 1) for i in range(size)])


def on_device(spectra, pair_remote, pair_count):
    windows, channels, width = spectra.shape
    bins = width // 2
    scale = 1.0 / math.sqrt(bins * windows)
    table = jnp.asarray(lag_table(bins))
    parity = (lax.axis_index("win") % 2).astype(jnp.int32)[None]

    other = core_swap(spectra)
    source = whiten_source(spectra)
    arrived = [route_swap(source, move) for move in MOVES]
    own, sibling, pair_count = whiten_both(spectra, other, pair_count)
    arrived, pair_count = lax.optimization_barrier((arrived, pair_count))
    half = ROUTES // 2
    first, second = jnp.stack(arrived[:half]), jnp.stack(arrived[half:])

    up_first, down_first = chip_shift(first, 1), chip_shift(first, -1)
    run = functools.partial(correlate, parity, own, sibling, table=table, scale=scale)
    own_first = run([first])
    own_first, second = lax.optimization_barrier((own_first, second))
    up_second, down_second = chip_shift(second, 1), chip_shift(second, -1)
    own_first, up_first, down_first = lax.optimization_barrier((own_first, up_first, down_first))
    near_first = run([up_first, down_first])
    near_first, up_first, up_second, down_second = lax.optimization_barrier(
        (near_first, up_first, up_second, down_second)
    )
    far_first = chip_shift(up_first, 1)
    far_second = chip_shift(down_second, -1)
    near_second = run([up_second, down_second])
    near_second, far_first, far_second = lax.optimization_barrier(
        (near_second, far_first, far_second)
    )
    c_far = run([far_first, far_second])
    c_far, second, near_first, near_second = lax.optimization_barrier(
        (c_far, second, near_first, near_second)
    )
    c_own = jnp.concatenate([own_first, run([second])])
    c_up = jnp.concatenate([near_first[:half], near_second[:half]])
    c_down = jnp.concatenate([near_first[half:], near_second[half:]])

    chips = lax.axis_size("win") // 2
    chip = lax.axis_index("win") // 2
    home = [c_own, chip_shift(c_down, 1), chip_shift(c_far, 2), chip_shift(c_up, -1)]
    stacked = jnp.stack(home)
    order = (chip - jnp.arange(chips)) % chips
    stacked = stacked[order]
    blocks = jnp.swapaxes(stacked, 0, 1).reshape(ROUTES, chips * 2 * channels, LAGS)
    back = [route_swap(blocks[i], move, back=True) for i, move in enumerate(MOVES)]

    here, sign = lax.axis_index("chan"), 1 - 2 * parity[0]
    live = jnp.arange(pair_remote.shape[1], dtype=jnp.int32) < pair_count[0]
    result = jnp.zeros((pair_remote.shape[1],) + back[0].shape, jnp.float32)
    for block, move in zip(back, MOVES):
        chosen = (live & (pair_remote[0] == here + move * sign))[:, None, None]
        result = jnp.where(chosen, block[None].astype(jnp.float32), result)
    return result[None, None]


def solution(mesh):
    in_specs = (P(None, ("chan", "win"), None), P("chan", None), P("chan"))
    out_specs = P("win", "chan", None, None, None)
    return jax.shard_map(
        on_device, mesh=mesh, in_specs=in_specs, out_specs=out_specs, check_vma=False
    )
```

```python
import functools
import math

import jax
import jax.numpy as jnp
import ml_dtypes
import numpy as np
from jax import lax
from jax.experimental import pallas as pl
from jax.experimental.pallas import tpu as pltpu
from jax.sharding import PartitionSpec as P

BAND = 64
LAGS = 256
REACH = 2
VMEM = 12 * 2**20
WIDE = 48 * 2**20
MOVES = (1, 2, -1, -2)
ROUTES = len(MOVES)


def lag_table(bins):
    t = np.arange(LAGS) - LAGS // 2
    f = np.arange(bins)
    angle = ((f[:, None] * t[None, :]) % (2 * bins)) * (math.pi / bins)
    table = np.concatenate([np.cos(angle), -np.sin(angle)], axis=0)
    return table.astype(np.float32).astype(ml_dtypes.bfloat16)


def band_matrix():
    row = lax.broadcasted_iota(jnp.int32, (128, 128), 0) // BAND
    column = lax.broadcasted_iota(jnp.int32, (128, 128), 1) // BAND
    return jnp.where(row == column, 1.0, 0.0).astype(jnp.bfloat16)


def whiten_rows(values):
    ones = band_matrix()
    rows, width = values.shape
    bins = width // 2
    parts = bins // 128
    split = [
        (values[:, i * 128 : (i + 1) * 128], values[:, bins + i * 128 : bins + (i + 1) * 128])
        for i in range(parts)
    ]
    powers = [re * re + im * im for re, im in split]
    stacked = jnp.concatenate([p * lax.rsqrt(jnp.maximum(p, 1e-30)) for p in powers], axis=0)
    high = stacked.astype(jnp.bfloat16)
    low = (stacked - high.astype(jnp.float32)).astype(jnp.bfloat16)
    total = jnp.dot(
        jnp.concatenate([high, low], axis=1),
        jnp.concatenate([ones, ones], axis=0),
        preferred_element_type=jnp.float32,
    )
    inverse = 1.0 / (total * (1.0 / BAND) + 1e-06)
    scaled = [inverse[i * rows : (i + 1) * rows] for i in range(parts)]
    real = [re * k for (re, _), k in zip(split, scaled)]
    imag = [im * k for (_, im), k in zip(split, scaled)]
    return jnp.concatenate(real + imag, axis=1).astype(jnp.bfloat16)


def source_kernel(spectra, out, held, done):
    windows = spectra.shape[0]
    copies = [pltpu.make_async_copy(spectra.at[w], held.at[w], done.at[w]) for w in range(windows)]
    for copy in copies:
        copy.start()
    rows = []
    for w, copy in enumerate(copies):
        copy.wait()
        rows.append(held[w].astype(jnp.float32)[0:1])
    out[...] = whiten_rows(jnp.concatenate(rows, axis=0))


def whiten_kernel(flag, own, sibling, own_out, sibling_out, flag_out, held, done):
    windows = own.shape[0]
    pairs = ((own, own_out), (sibling, sibling_out))

    def fetch(k, w):
        return pltpu.make_async_copy(pairs[k][0].at[w], held.at[k, w], done.at[k, w])

    for w in range(windows):
        for k in range(2):
            fetch(k, w).start()

    def body(w, carry):
        for k in range(2):
            fetch(k, w).wait()
            pairs[k][1][w] = whiten_rows(held[k, w].astype(jnp.float32))
        return carry

    lax.fori_loop(0, windows, body, 0)
    flag_out[0] = flag[0]


def whiten_source(spectra):
    windows, _, width = spectra.shape
    return pl.pallas_call(
        source_kernel,
        in_specs=[pl.BlockSpec(memory_space=pltpu.HBM)],
        out_specs=pl.BlockSpec(memory_space=pltpu.VMEM),
        scratch_shapes=[
            pltpu.VMEM(spectra.shape, spectra.dtype),
            pltpu.SemaphoreType.DMA((windows,)),
        ],
        out_shape=jax.ShapeDtypeStruct((windows, width), jnp.bfloat16),
        compiler_params=pltpu.CompilerParams(vmem_limit_bytes=VMEM),
        cost_estimate=pl.CostEstimate(flops=10**6, bytes_accessed=2 * 2**20, transcendentals=0),
        name="whiten_source",
    )(spectra)


def whiten_both(own, sibling, flag):
    windows = own.shape[0]
    shape = jax.ShapeDtypeStruct(own.shape, jnp.bfloat16)
    scalar, whole = pl.BlockSpec(memory_space=pltpu.SMEM), pl.BlockSpec(memory_space=pltpu.VMEM)
    return pl.pallas_call(
        whiten_kernel,
        in_specs=[scalar] + [pl.BlockSpec(memory_space=pltpu.HBM)] * 2,
        out_specs=[whole, whole, scalar],
        out_shape=[shape, shape, jax.ShapeDtypeStruct(flag.shape, flag.dtype)],
        scratch_shapes=[
            pltpu.VMEM((2,) + own.shape, own.dtype),
            pltpu.SemaphoreType.DMA((2, windows)),
        ],
        compiler_params=pltpu.CompilerParams(vmem_limit_bytes=VMEM),
        cost_estimate=pl.CostEstimate(flops=10**9, bytes_accessed=8 * 2**20, transcendentals=0),
        name="whiten_both",
    )(flag, own, sibling)


def correlate_kernel(groups, scale, parity, *refs):
    own, sib = refs[:2]
    sources = refs[2 : 2 + groups]
    table_hbm, out, prod_r, prod_i, src_r, src_i, src_s, table, done = refs[2 + groups :]
    fetch = pltpu.make_async_copy(table_hbm, table, done)
    fetch.start()
    windows, half, width = own.shape
    bins = width // 2
    per = sources[0].shape[0]
    for g, ref in enumerate(sources):
        rows = slice(g * per, (g + 1) * per)
        a, b = ref[:, :, :bins].astype(jnp.float32), ref[:, :, bins:].astype(jnp.float32)
        src_r[rows] = a
        src_i[rows] = b
        src_s[rows] = a + b

    def body(q, carry):
        lanes = pl.ds(pl.multiple_of(q * 128, 128), 128)
        upper = pl.ds(pl.multiple_of(bins + q * 128, 128), 128)
        for h, ref in enumerate((own, sib)):
            place = (parity[0] + h) % 2
            for t in range(0, half, 8):
                chan = []
                for w in range(windows):
                    x = ref[w, :, lanes].astype(jnp.float32)[t : t + 8]
                    y = ref[w, :, upper].astype(jnp.float32)[t : t + 8]
                    chan.append((x, x + y, x - y))
                for s in range(groups * per):
                    total = None
                    for w in range(windows):
                        terms = [
                            jnp.broadcast_to(r[s, w : w + 1, lanes], (8, 128)) * c
                            for r, c in zip((src_s, src_r, src_i), chan[w])
                        ]
                        total = terms if total is None else [p + q for p, q in zip(total, terms)]
                    tile = (s * 2 + place) * (half // 8) + t // 8
                    prod_r[tile, :, lanes] = (total[0] - total[2]).astype(jnp.bfloat16)
                    prod_i[tile, :, lanes] = (total[0] - total[1]).astype(jnp.bfloat16)
        return carry

    def rows(ref):
        return ref[...].reshape(ref.shape[0] * 8, bins)

    lax.fori_loop(0, bins // 128, body, 0)
    fetch.wait()
    total = jnp.dot(rows(prod_r), table[:bins], preferred_element_type=jnp.float32) + jnp.dot(
        rows(prod_i), table[bins:], preferred_element_type=jnp.float32
    )
    out[...] = (total * scale).reshape(out.shape).astype(out.dtype)


def correlate(parity, own, sibling, sources, table, scale):
    windows, half, width = own.shape
    bins = width // 2
    groups, per = len(sources), sources[0].shape[0]
    n = groups * per
    whole = pl.BlockSpec(memory_space=pltpu.VMEM)
    return pl.pallas_call(
        functools.partial(correlate_kernel, groups, scale),
        in_specs=[pl.BlockSpec(memory_space=pltpu.SMEM)] + [whole] * (2 + groups)
        + [pl.BlockSpec(memory_space=pltpu.HBM)],
        out_specs=whole,
        out_shape=jax.ShapeDtypeStruct((n, 2 * half, LAGS), jnp.bfloat16),
        scratch_shapes=[
            pltpu.VMEM((n * 2 * half // 8, 8, bins), jnp.bfloat16),
            pltpu.VMEM((n * 2 * half // 8, 8, bins), jnp.bfloat16),
            pltpu.VMEM((n, windows, bins), jnp.float32),
            pltpu.VMEM((n, windows, bins), jnp.float32),
            pltpu.VMEM((n, windows, bins), jnp.float32),
            pltpu.VMEM(table.shape, table.dtype),
            pltpu.SemaphoreType.DMA,
        ],
        compiler_params=pltpu.CompilerParams(vmem_limit_bytes=WIDE),
        cost_estimate=pl.CostEstimate(
            flops=n * 10**9, bytes_accessed=8 * 2**20, transcendentals=0
        ),
        name=f"correlate_{n}",
    )(parity, own, sibling, *sources, table)


def route_swap(block, move, back=False):
    blocks, size = lax.axis_size("chan"), lax.axis_size("win")
    pairs = []
    for w in range(size):
        for b in range(blocks):
            to = b - move if w % 2 else b + move
            inside = 0 <= to < blocks
            pairs.append((w * blocks + b, w * blocks + to if inside else (w ^ 1) * blocks + b))
    return lax.ppermute(block, ("win", "chan"), [(j, i) if back else (i, j) for i, j in pairs])


def chip_shift(block, distance):
    size = lax.axis_size("win")
    return lax.ppermute(block, "win", [(i, (i + 2 * distance) % size) for i in range(size)])


def core_swap(block):
    size = lax.axis_size("win")
    return lax.ppermute(block, "win", [(i, i ^ 1) for i in range(size)])


def on_device(spectra, pair_remote, pair_count):
    windows, channels, width = spectra.shape
    bins = width // 2
    scale = 1.0 / math.sqrt(bins * windows)
    table = jnp.asarray(lag_table(bins))
    parity = (lax.axis_index("win") % 2).astype(jnp.int32)[None]

    other = core_swap(spectra)
    source = whiten_source(spectra)
    arrived = [route_swap(source, move) for move in MOVES]
    own, sibling, pair_count = whiten_both(spectra, other, pair_count)
    arrived, pair_count = lax.optimization_barrier((arrived, pair_count))
    half = ROUTES // 2
    first, second = jnp.stack(arrived[:half]), jnp.stack(arrived[half:])

    up_first, down_first = chip_shift(first, 1), chip_shift(first, -1)
    run = functools.partial(correlate, parity, own, sibling, table=table, scale=scale)
    own_first = run([first])
    own_first, second = lax.optimization_barrier((own_first, second))
    up_second, down_second = chip_shift(second, 1), chip_shift(second, -1)
    own_first, up_first, down_first = lax.optimization_barrier((own_first, up_first, down_first))
    near_first = run([up_first, down_first])
    near_first, down_first, up_second, down_second = lax.optimization_barrier(
        (near_first, down_first, up_second, down_second)
    )
    far_first = chip_shift(down_first, -1)
    far_second = chip_shift(up_second, 1)
    near_second = run([up_second, down_second])
    near_second, far_first, far_second = lax.optimization_barrier(
        (near_second, far_first, far_second)
    )
    c_far = run([far_first, far_second])
    c_far, second, near_first, near_second = lax.optimization_barrier(
        (c_far, second, near_first, near_second)
    )
    c_own = jnp.concatenate([own_first, run([second])])
    c_up = jnp.concatenate([near_first[:half], near_second[:half]])
    c_down = jnp.concatenate([near_first[half:], near_second[half:]])

    chips = lax.axis_size("win") // 2
    chip = lax.axis_index("win") // 2
    home = [c_own, chip_shift(c_down, 1), chip_shift(c_far, 2), chip_shift(c_up, -1)]
    stacked = jnp.stack(home)
    order = (chip - jnp.arange(chips)) % chips
    stacked = stacked[order]
    blocks = jnp.swapaxes(stacked, 0, 1).reshape(ROUTES, chips * 2 * channels, LAGS)
    back = [route_swap(blocks[i], move, back=True) for i, move in enumerate(MOVES)]

    here, sign = lax.axis_index("chan"), 1 - 2 * parity[0]
    live = jnp.arange(pair_remote.shape[1], dtype=jnp.int32) < pair_count[0]
    result = jnp.zeros((pair_remote.shape[1],) + back[0].shape, jnp.float32)
    for block, move in zip(back, MOVES):
        chosen = (live & (pair_remote[0] == here + move * sign))[:, None, None]
        result = jnp.where(chosen, block[None].astype(jnp.float32), result)
    return result[None, None]


def solution(mesh):
    in_specs = (P(None, ("chan", "win"), None), P("chan", None), P("chan"))
    out_specs = P("win", "chan", None, None, None)
    return jax.shard_map(
        on_device, mesh=mesh, in_specs=in_specs, out_specs=out_specs, check_vma=False
    )
```
